32 devices in a mesh: section: 2 (over y), expert: 16 (over z, x, core).
Axes of the slice: x: 2, y: 2, z: 4, core: 2. Of those that a mesh axis runs over, the one named last changes fastest.
Arguments:
- section_input: bfloat16 [2, 2048, 2880], P('section', 'expert'), may hold values from -6 to 6
- attention_gain: float32 [2, 2880], P('section'), may hold values from 0.1 to 1.9
- query_key_value_weight: bfloat16 [2, 2880, 2560], P('section', 'expert'), may hold values from -0.109375 to 0.109375
- qkv_bias: float32 [2, 2560], P('section'), may hold values from -3 to 8
- out_weight: bfloat16 [2, 2048, 2880], P('section'), may hold values from -0.125 to 0.125
- out_bias: float32 [2, 2880], P('section'), may hold values from -3 to 3
- attention_sink_logits: float32 [2, 32], P('section'), may hold values from -1 to 250
- expert_gain: float32 [2, 2880], P('section'), may hold values from 0.1 to 1.9
- gate_up_weight: bfloat16 [2, 16, 2880, 1440], P('section', 'expert'), may hold values from -0.109375 to 0.109375
- down_weight: bfloat16 [2, 16, 720, 2880], P('section', 'expert'), may hold values from -0.15625 to 0.15625
- expert_ids: int32 [2, 2048, 4], P('section', 'expert'), may hold values from 0 to 7, all different within a row; in each aligned block of 128 rows (0 to 127, 128 to 255, ..., all dimensions but the last counted through in order) at most 80 rows name the same one
- gate_logits: float32 [2, 2048, 4], P('section', 'expert'), may hold values from -8 to 204
- placement: int32 [2, 8], P('section'), may hold values from 0 to 7, each once within a row
Outputs:
- section_output: bfloat16 [2, 2048, 2880], P('section', 'expert')
The draws below stay inside these ranges and needn't reach their ends.
Inputs may be any that keep to these rules, and one draw needn't show every extreme that they name: `expert_ids`: within each section, among the 128 tokens of one device no expert is named more than 80 times, a bound that some block reaches. `placement`: each row names every expert once.
All inputs are finite; a program needn't handle non-finite values.
Results may differ from the reference program's by a relative error of at most 0.018.
Values may be sent and summed in bfloat16 or wider, within the bound.
No kernel may reach another device: no remote copies, remote signals or barrier semaphores. Data moves between devices by JAX's collectives and lax.ppermute only.
A program may use at most 128 MiB of HBM per device.

```python
import math
import jax
import jax.numpy as jnp
import numpy as np
from jax import lax

MODEL_DIM = 2880
HEAD_DIM = 64
QUERY_HEADS = 32
KEY_VALUE_HEADS = 4
WINDOW_TOKENS = 128
HID = 1440
TOP = 4
TOK_DEV = 128
SEQUENCE_TOKENS = 2048
EXPERTS = 8
HID_DEV = 720
CAP = 80
N_SECTION = 2
N_EXPERT = 16


def draw_attention_sink_logits(key, part):
    key_portions = jax.random.split(key, 1)
    tensor_shape = (N_SECTION, QUERY_HEADS)
    gentle = jax.random.uniform(key_portions[0], tensor_shape, jnp.float32, -1.0, 4.0)
    return gentle


def draw_qkv_bias(key, part):
    key_portions = jax.random.split(key, 1)
    tensor_shape = (N_SECTION, (QUERY_HEADS + 2 * KEY_VALUE_HEADS) * HEAD_DIM)
    return 0.5 * jax.random.truncated_normal(key_portions[0], -6.0, 6.0, tensor_shape, jnp.float32)


def draw_gate_logits(key, part):
    key_portions = jax.random.split(key, 1)
    tensor_shape = (N_SECTION, SEQUENCE_TOKENS, TOP)
    return 1.5 * jax.random.truncated_normal(key_portions[0], -5.0, 5.0, tensor_shape, jnp.float32)


def level_of(rng, extent, cuts, smallest, high):
    factor_of, own = 1.0, jax.random.fold_in(rng, 6)
    for axis_at, parts in cuts:
        draws = jnp.exp(jax.random.uniform(jax.random.fold_in(own, axis_at), (parts,), jnp.float32, smallest / len(cuts), high / len(cuts)))
        factor_of = factor_of * jnp.repeat(draws, extent[axis_at] // parts).reshape([-1 if axis == axis_at else 1 for axis in range(len(extent))])
    return factor_of


def routed_block(own_key, own, number, rows, number_of, top, limit, skew):
    ranking = jax.random.permutation(own_key, number_of)
    heavy_load, ordinary = load_shares(number_of, rows * top, limit, skew, True), load_shares(number_of, rows * top, limit, skew, False)
    places = jnp.arange(number_of)

    def named(sizes, rotation):
        used = int((sizes > 0).sum())
        fixed = max(1, used // 4)
        passed = fixed + (places - fixed + rotation * (used - fixed)) % max(1, number_of - fixed)
        return jnp.zeros((number_of,), jnp.int32).at[ranking[jnp.where(places < fixed, places, passed)]].set(jnp.asarray(sizes, jnp.int32))

    sizes = jnp.where(number % 4 == 0, named(heavy_load, number // 4), named(ordinary, number - number // 4 - 1))
    mixed = jax.random.permutation(jax.random.fold_in(own, 3), number_of)
    source_of, taker = mixed[0:number_of // 2 * 2:2], mixed[1:number_of // 2 * 2:2]
    room = jnp.minimum(sizes[source_of] - 1, limit - sizes[taker]) // 2
    room = jnp.where((source_of == ranking[0]) | (taker == ranking[0]) | (sizes[taker] == 0), 0, jnp.maximum(room, 0))
    passed = jax.random.randint(jax.random.fold_in(own, 4), (number_of // 2,), 0, 1 << 20) % (room + 1)
    sizes = sizes.at[source_of].add(-passed).at[taker].add(passed)
    members = jnp.searchsorted(jnp.cumsum(sizes), jnp.arange(rows * top), side="right").astype(jnp.int32)
    table = members.reshape(top, rows).T
    table = table[jax.random.permutation(jax.random.fold_in(own, 1), rows)]
    rotation = jax.random.randint(jax.random.fold_in(own, 2), (rows, 1), 0, top)
    return jnp.take_along_axis(table, (jnp.arange(top)[None, :] + rotation) % top, axis=1)


def load_shares(number_of, total, limit, lean, full):
    loads = [(1 << 20) // math.isqrt(grade ** lean) + 1 for grade in range(1, number_of + 1)]
    largest = limit if full else min(limit, max(-(-total // number_of), total * loads[0] // sum(loads)))
    least = 1 if total - largest >= number_of - 1 else 0
    given, surplus = [largest] + [least] * (number_of - 1), total - largest - least * (number_of - 1)
    while surplus > 0:
        candidates = [i for i in range(1, number_of) if given[i] < largest] or [i for i in range(1, number_of) if given[i] < limit]
        whole, remaining = sum([loads[i] for i in candidates]), surplus
        for i in candidates:
            addition = min(limit - given[i], max(1, remaining * loads[i] // whole), surplus)
            given[i] = given[i] + addition
            surplus = surplus - addition
    return np.array(given)


def centred(stream_key, dims, deviation, reach, shards=(), held_as=jnp.bfloat16):
    gain = level_of(stream_key, dims, shards, -0.22, 0.18) if shards else 1.0
    drawn = jax.random.normal(stream_key, dims, jnp.float32) * deviation * gain
    return jnp.minimum(jnp.maximum(drawn, -reach), reach).astype(held_as)


def setup_inputs(seed: int = 0) -> dict:
    splits = jax.random.split(jax.random.key(seed), 14)
    section_input = centred(splits[0], (N_SECTION, SEQUENCE_TOKENS, MODEL_DIM), 1.0, 6.0, ((0, 2), (1, 16)))
    attention_gain = jnp.clip(1.0 + 0.18 * jax.random.normal(splits[1], (N_SECTION, MODEL_DIM), jnp.float32), 0.1, 1.9)
    query_key_value_weight = centred(splits[2], (N_SECTION, MODEL_DIM, (QUERY_HEADS + 2 * KEY_VALUE_HEADS) * HEAD_DIM), MODEL_DIM ** -0.5, 0.109375, ((0, 2), (1, 16)))
    qkv_bias = draw_qkv_bias(jax.random.fold_in(splits[13], 71), 0)
    out_weight = centred(splits[4], (N_SECTION, QUERY_HEADS * HEAD_DIM, MODEL_DIM), (QUERY_HEADS * HEAD_DIM) ** -0.5, 0.125, ((0, 2),))
    out_bias = centred(splits[5], (N_SECTION, MODEL_DIM), 0.5, 3.0, ((0, 2),), jnp.float32)
    attention_sink_logits = draw_attention_sink_logits(jax.random.fold_in(splits[13], 71), 0)
    expert_gain = jnp.clip(1.0 + 0.18 * jax.random.normal(splits[7], (N_SECTION, MODEL_DIM), jnp.float32), 0.1, 1.9)
    gate_up_weight = centred(splits[8], (N_SECTION, N_EXPERT, MODEL_DIM, 2 * HID_DEV), MODEL_DIM ** -0.5, 0.109375, ((0, 2), (1, 16)))
    down_weight = centred(splits[9], (N_SECTION, N_EXPERT, HID_DEV, MODEL_DIM), HID ** -0.5, 0.15625, ((0, 2), (1, 16)))
    expert_ids_keys = jax.random.split(jax.random.fold_in(splits[10], 1), N_SECTION * SEQUENCE_TOKENS // TOK_DEV)
    expert_ids_turns = jax.random.permutation(jax.random.fold_in(splits[10], 3), N_SECTION * SEQUENCE_TOKENS // TOK_DEV)
    expert_ids = jax.vmap(lambda own, number: routed_block(jax.random.fold_in(splits[10], 2), own, number, TOK_DEV, EXPERTS, TOP, CAP, 2))(expert_ids_keys, expert_ids_turns).reshape((N_SECTION, SEQUENCE_TOKENS, TOP))
    gate_logits = draw_gate_logits(jax.random.fold_in(splits[13], 71), 0)
    placement = jax.vmap(lambda own: jax.random.permutation(own, EXPERTS))(jax.random.split(splits[12], N_SECTION)).reshape((N_SECTION, EXPERTS)).astype(jnp.int32)
    return dict(section_input=section_input, attention_gain=attention_gain, query_key_value_weight=query_key_value_weight, qkv_bias=qkv_bias, out_weight=out_weight, out_bias=out_bias, attention_sink_logits=attention_sink_logits, expert_gain=expert_gain, gate_up_weight=gate_up_weight, down_weight=down_weight, expert_ids=expert_ids, gate_logits=gate_logits, placement=placement)


def normed(vector, gain_row):
    as_float = vector.astype(jnp.float32)
    inverse_rms = lax.rsqrt(lax.optimization_barrier(jnp.mean(as_float * as_float, axis=-1, keepdims=True)) + 1e-05)
    return (as_float * inverse_rms * gain_row).astype(jnp.bfloat16)

def attend(projected_rows, sink_logit_row):
    query_group_width = QUERY_HEADS // KEY_VALUE_HEADS
    count_of_blocks = SEQUENCE_TOKENS // WINDOW_TOKENS
    query_rows = projected_rows[:, :QUERY_HEADS * HEAD_DIM].reshape(count_of_blocks, WINDOW_TOKENS, KEY_VALUE_HEADS, query_group_width, HEAD_DIM).astype(jnp.float32)
    key_columns = projected_rows[:, QUERY_HEADS * HEAD_DIM:QUERY_HEADS * HEAD_DIM + KEY_VALUE_HEADS * HEAD_DIM].reshape(SEQUENCE_TOKENS, KEY_VALUE_HEADS, HEAD_DIM)
    value_columns = projected_rows[:, QUERY_HEADS * HEAD_DIM + KEY_VALUE_HEADS * HEAD_DIM:].reshape(SEQUENCE_TOKENS, KEY_VALUE_HEADS, HEAD_DIM)

    def banded(source_rows):
        padded_rows = jnp.concatenate([jnp.zeros((WINDOW_TOKENS, KEY_VALUE_HEADS, HEAD_DIM), source_rows.dtype), source_rows], 0)
        preceding_rows = padded_rows[:SEQUENCE_TOKENS].reshape(count_of_blocks, WINDOW_TOKENS, KEY_VALUE_HEADS, HEAD_DIM)
        return jnp.concatenate([preceding_rows, source_rows.reshape(count_of_blocks, WINDOW_TOKENS, KEY_VALUE_HEADS, HEAD_DIM)], 1).astype(jnp.float32)
    key_row_slice = banded(key_columns)
    value_row_slice = banded(value_columns)
    scores = jnp.einsum('bikgd,bjkd->bkgij', query_rows, key_row_slice) * 0.125
    query_idx = jnp.arange(WINDOW_TOKENS).astype(jnp.int32)[:, None]
    key_idx = jnp.arange(2 * WINDOW_TOKENS).astype(jnp.int32)[None, :]
    key_start = (jnp.arange(count_of_blocks).astype(jnp.int32) * WINDOW_TOKENS - WINDOW_TOKENS)[:, None, None]
    distance = query_idx - key_idx + WINDOW_TOKENS
    inside = (distance >= 0) & (distance < WINDOW_TOKENS) & (key_start + key_idx >= 0)
    inside = inside[:, None, None, :, :]
    head_sink_logit = sink_logit_row.reshape(KEY_VALUE_HEADS, query_group_width)[None, :, :, None]
    masked = jnp.where(inside, scores, -1e+30)
    peak = jnp.maximum(lax.optimization_barrier(jnp.max(masked, axis=-1)), head_sink_logit)
    numer = jnp.where(inside, jnp.exp(masked - peak[..., None]), 0.0)
    denominator = lax.optimization_barrier(jnp.sum(numer, axis=-1)) + jnp.exp(head_sink_logit - peak)
    attention = (numer / denominator[..., None]).astype(jnp.bfloat16)
    mixed = jnp.einsum('bkgij,bjkd->bikgd', attention.astype(jnp.float32), value_row_slice)
    return mixed.astype(jnp.bfloat16).reshape(SEQUENCE_TOKENS, QUERY_HEADS * HEAD_DIM)

def swiglu(hidden):
    gate_part = hidden[:, :HID_DEV]
    up_part = hidden[:, HID_DEV:]
    return ((up_part + 1.0) * gate_part * jax.nn.sigmoid(1.702 * gate_part)).astype(jnp.bfloat16)

def experts(normed_mid, chosen, logits, holders, gate_up_weight, down_weight):
    flat_ids = chosen.reshape(N_EXPERT, TOK_DEV * TOP)
    one_hot = (flat_ids[:, :, None] == jnp.arange(EXPERTS).astype(jnp.int32)[None, None, :]).astype(jnp.int32)
    slot_of = lax.optimization_barrier(jnp.sum((jnp.cumsum(one_hot, axis=1) - 1) * one_hot, axis=-1))
    block_index = jnp.arange(N_EXPERT).astype(jnp.int32)[:, None]
    where_row = (block_index * CAP + slot_of).reshape(-1).astype(jnp.int32)
    token_of = (block_index * TOK_DEV + jnp.arange(TOK_DEV * TOP).astype(jnp.int32)[None, :] // TOP).reshape(-1).astype(jnp.int32)
    source_rows = jnp.full((EXPERTS, N_EXPERT * CAP), -1, jnp.int32).at[chosen.reshape(-1), where_row].set(token_of)
    matches = (holders[:, None] == jnp.arange(EXPERTS).astype(jnp.int32)[None, :]).astype(jnp.int32)
    holder_of = lax.optimization_barrier(jnp.sum(jnp.arange(EXPERTS).astype(jnp.int32)[:, None] * matches, axis=0)).astype(jnp.int32)

    def one_expert(expert_index):
        row_ids = source_rows[expert_index]
        valid_rows = (row_ids >= 0)[:, None].astype(jnp.bfloat16)
        rows_in = jnp.take(normed_mid, jnp.maximum(row_ids, 0), axis=0) * valid_rows
        pair_slot = holder_of[expert_index]
        accumulated = jnp.zeros((N_EXPERT * CAP, MODEL_DIM), jnp.float32)
        for tile_index in range(2):
            tile_gu = gate_up_weight[2 * pair_slot + tile_index]
            tile_down = down_weight[2 * pair_slot + tile_index]
            tile_act = swiglu(jnp.dot(rows_in, tile_gu, preferred_element_type=jnp.float32))
            tile_part = jnp.dot(tile_act, tile_down, preferred_element_type=jnp.float32).astype(jnp.bfloat16)
            tile_part = lax.optimization_barrier(tile_part)
            accumulated = accumulated + tile_part.astype(jnp.float32)
        return accumulated.astype(jnp.bfloat16)
    results = lax.map(one_expert, jnp.arange(EXPERTS).astype(jnp.int32))
    picked = results[chosen.reshape(-1), where_row].reshape(SEQUENCE_TOKENS, TOP, MODEL_DIM)
    picked = lax.optimization_barrier(picked).astype(jnp.float32)
    gate_weights = jax.nn.softmax(logits, axis=-1)
    return lax.optimization_barrier(jnp.sum(picked * gate_weights[..., None], axis=1))

def reference(section_input, attention_gain, query_key_value_weight, qkv_bias, out_weight, out_bias, attention_sink_logits, expert_gain, gate_up_weight, down_weight, expert_ids, gate_logits, placement):
    collected = []
    for section_index in range(N_SECTION):
        state = section_input[section_index]
        normed_in = normed(state, attention_gain[section_index])
        projected_rows = (jnp.dot(normed_in, query_key_value_weight[section_index], preferred_element_type=jnp.float32) + qkv_bias[section_index]).astype(jnp.bfloat16)
        attended = attend(projected_rows, attention_sink_logits[section_index])
        residual = (state.astype(jnp.float32) + jnp.dot(attended, out_weight[section_index], preferred_element_type=jnp.float32) + out_bias[section_index]).astype(jnp.bfloat16)
        normed_mid = normed(residual, expert_gain[section_index])
        mixture = experts(normed_mid, expert_ids[section_index], gate_logits[section_index], placement[section_index], gate_up_weight[section_index], down_weight[section_index])
        collected.append((residual.astype(jnp.float32) + mixture).astype(jnp.bfloat16))
    return jnp.roll(jnp.stack(collected), 1, axis=0)
```

```python
import functools

import jax
import jax.numpy as jnp
from jax import lax
from jax.experimental import pallas as pl
from jax.experimental.pallas import tpu as pltpu
from jax.sharding import PartitionSpec as P

HEAD_DIM = 64
QUERY_HEADS = 32
KEY_VALUE_HEADS = 4
WINDOW_TOKENS = 128
TOP = 4
GROUP = QUERY_HEADS // KEY_VALUE_HEADS
QUERY_COLS = GROUP * HEAD_DIM
GROUP_COLS = QUERY_COLS + 2 * HEAD_DIM
BF16 = jnp.bfloat16
F32 = jnp.float32
VMEM_BYTES = 50 * 1024 * 1024


def swap(x, mask):
    size = lax.axis_size("expert")
    return lax.ppermute(x, "expert", [(i, i ^ mask) for i in range(size)])


def normed(vector, gain_row):
    as_float = vector.astype(F32)
    inverse_rms = lax.rsqrt(jnp.mean(as_float * as_float, axis=-1, keepdims=True) + 1e-05)
    return (as_float * inverse_rms * gain_row).astype(BF16)


def params(limit=VMEM_BYTES):
    return pltpu.CompilerParams(vmem_limit_bytes=limit)


SMEM_SPEC = pl.BlockSpec(memory_space=pltpu.SMEM)
VMEM_SPEC = pl.BlockSpec(memory_space=pltpu.VMEM)


def project_half(which, own, core, first, tokens, mine, theirs, depth):
    total = None
    for r in range(4):
        first_core = jnp.where(core == 0, mine[r], theirs[r])
        second_core = jnp.where(core == 0, theirs[r], mine[r])
        both = jnp.concatenate([first_core, second_core], axis=0)
        start = pl.multiple_of((which * 4 + (own ^ r)) * 2 * depth, 128)
        columns = pl.ds(start, 2 * depth)
        stacked = jnp.concatenate([t[:, columns] for t in tokens], axis=0)
        part = jnp.dot(stacked, both, preferred_element_type=F32)
        total = part if total is None else total + part
    return total if first is None else total + first


def project_near(depth, where, t0, t1, t2, t3, mine, theirs, out):
    half, own, core = where[0], where[1], where[2]
    out[...] = project_half(half, own, core, None, (t0, t1, t2, t3), mine, theirs, depth)


def project_far(depth, where, t0, t1, t2, t3, mine, theirs, near, bias, queries, keyvals):
    half, own, core = where[0], where[1], where[2]
    total = project_half(
        1 - half, own, core, near[...], (t0, t1, t2, t3), mine, theirs, depth
    )
    rows = t0.shape[0]
    projected = (total + bias[pl.ds(own, 1), :]).astype(BF16)
    for r in range(4):
        block = projected[r * rows : (r + 1) * rows]
        queries[own ^ r] = block[:, :QUERY_COLS]
        keyvals[own ^ r] = block[:, QUERY_COLS:]


def attend(where, queries, keyvals, behind, sinks, out):
    half, own, core = where[0], where[1], where[2]
    rows = queries.shape[1]
    keys = 2 * rows
    shape = (GROUP * rows, keys)
    query_at = lax.rem(lax.broadcasted_iota(jnp.int32, shape, 0), rows)
    distance = query_at - lax.broadcasted_iota(jnp.int32, shape, 1) + rows
    band = (distance >= 0) & (distance < WINDOW_TOKENS)
    sink = jnp.concatenate(
        [jnp.full((rows, 1), sinks[own * GROUP + j], F32) for j in range(GROUP)], axis=0
    )
    for b in range(4):
        before = behind[b + core]
        now = keyvals[b]
        both = jnp.concatenate([before, now], axis=0)
        q = queries[b]
        stacked = jnp.concatenate(
            [q[:, j * HEAD_DIM : (j + 1) * HEAD_DIM] for j in range(GROUP)], axis=0
        )
        scores = (
            lax.dot_general(
                stacked,
                both[:, :HEAD_DIM],
                (((1,), (1,)), ((), ())),
                preferred_element_type=F32,
            )
            * 0.125
        )
        inside = band
        inside = band
        if b == 0:
            first_key = jnp.where((half == 0) & (core == 0), rows, 0)
            inside = band & (lax.broadcasted_iota(jnp.int32, shape, 1) >= first_key)
        masked = jnp.where(inside, scores, -1e30)
        peak = jnp.maximum(jnp.max(masked, axis=-1, keepdims=True), sink)
        numer = jnp.where(inside, jnp.exp(masked - peak), 0.0)
        denominator = jnp.sum(numer, axis=-1, keepdims=True) + jnp.exp(sink - peak)
        weights = (numer / denominator).astype(BF16)
        mixed = jnp.dot(weights, both[:, HEAD_DIM:], preferred_element_type=F32).astype(BF16)
        out[b] = jnp.concatenate(
            [mixed[j * rows : (j + 1) * rows] for j in range(GROUP)], axis=1
        )


def out_project(where, attended, weight, state, bias, gain, residual, mid, total):
    step = pl.program_id(0)

    @pl.when(step == 0)
    def _():
        total[...] = state[...].astype(F32) + bias[...]

    total[...] += jnp.dot(attended[0], weight[...], preferred_element_type=F32)

    @pl.when(step == 3)
    def _():
        kept = total[...].astype(BF16)
        residual[...] = kept
        mid[...] = normed(kept, gain[...])


def routing(ids, logits, experts, slots):
    gates = jax.nn.softmax(logits, axis=-1)
    hits = ids[None, :, :] == experts[:, None, None]
    chosen = jnp.any(hits, axis=-1)
    weight = jnp.sum(jnp.where(hits, gates[None], 0.0), axis=-1)
    rows = ids.shape[0]
    earlier = jnp.arange(rows)[:, None] < jnp.arange(rows)[None, :]
    rank = jnp.dot(chosen.astype(BF16), earlier.astype(BF16), preferred_element_type=F32)
    slot = jnp.arange(slots, dtype=jnp.int32)
    one_hot = (rank.astype(jnp.int32)[:, None, :] == slot[None, :, None]) & chosen[:, None, :]
    return one_hot.astype(BF16), weight


def packed(one_hot, rows):
    return jnp.einsum("rst,td->rsd", one_hot, rows, preferred_element_type=F32).astype(BF16)


def unpacked(one_hot, weight, results):
    spread = jnp.einsum("rst,rsd->rtd", one_hot, results, preferred_element_type=F32)
    return jnp.sum(spread * weight[:, :, None], axis=0)


def swiglu(hidden):
    half_cols = hidden.shape[1] // 2
    gate_part = hidden[:, :half_cols]
    up_part = hidden[:, half_cols:]
    return ((up_part + 1.0) * gate_part * jax.nn.sigmoid(1.702 * gate_part)).astype(BF16)


def expert(rows, tiles):
    shape = rows.shape
    flat = rows.reshape(-1, shape[-1])
    total = 0.0
    for gate_up, down in tiles:
        hidden = jnp.dot(flat, gate_up, preferred_element_type=F32)
        part = jnp.dot(swiglu(hidden), down, preferred_element_type=F32).astype(BF16)
        total = total + part.astype(F32)
    return total.astype(BF16).reshape(shape)


def spread_out(blocks):
    return [blocks[0]] + [swap(blocks[r], 2 * r) for r in range(1, 4)]


def shards(
    section_input,
    attention_gain,
    query_key_value_weight,
    qkv_bias,
    out_weight,
    out_bias,
    attention_sink_logits,
    expert_gain,
    gate_up_weight,
    down_weight,
    expert_ids,
    gate_logits,
    placement,
):
    rows, width = section_input.shape[1:]
    experts_count = placement.shape[1]
    slots = 2 * min(rows // 2, rows * TOP * 5 // (8 * experts_count))
    me = lax.axis_index("expert").astype(jnp.int32)
    half, own, core = me >> 3, (me >> 1) & 3, me & 1
    where = jnp.stack([half, own, core])
    state = section_input[0]

    weight = query_key_value_weight[0]
    weight_rows = weight.shape[0]
    depth = -(-weight_rows // 64) * 64
    query_end = QUERY_HEADS * HEAD_DIM
    key_end = query_end + KEY_VALUE_HEADS * HEAD_DIM

    def grouped(array):
        lead = array.shape[0]
        return jnp.concatenate(
            [
                array[:, :query_end].reshape(lead, 4, QUERY_COLS),
                array[:, query_end:key_end].reshape(lead, 4, HEAD_DIM),
                array[:, key_end:].reshape(lead, 4, HEAD_DIM),
            ],
            axis=2,
        )

    by_group = jnp.pad(grouped(weight).transpose(1, 0, 2), ((0, 0), (0, depth - weight_rows), (0, 0)))
    bias = grouped(qkv_bias)[0]
    pick = lambda array, r: lax.dynamic_index_in_dim(array, own ^ r, 0, keepdims=False)
    near_mine = jnp.stack(spread_out([pick(by_group, r) for r in range(4)]))
    far_mine = swap(near_mine, 8)
    near_theirs = swap(near_mine, 1)
    far_theirs = swap(far_mine, 1)

    size = lax.axis_size("expert")
    normed_in = normed(state, attention_gain[0])
    blocked = jnp.pad(
        normed_in.reshape(rows, size, width // size), ((0, 0), (0, 0), (0, depth - width // size))
    ).reshape(rows, size * depth)
    tokens = spread_out([blocked] * 4)

    near = pl.pallas_call(
        functools.partial(project_near, depth),
        out_shape=jax.ShapeDtypeStruct((4 * rows, GROUP_COLS), F32),
        in_specs=[SMEM_SPEC] + [VMEM_SPEC] * 6,
        out_specs=VMEM_SPEC,
        compiler_params=params(),
        name="project_near",
    )(where, *tokens, near_mine, near_theirs)
    queries, keyvals = pl.pallas_call(
        functools.partial(project_far, depth),
        out_shape=(
            jax.ShapeDtypeStruct((4, rows, QUERY_COLS), BF16),
            jax.ShapeDtypeStruct((4, rows, 2 * HEAD_DIM), BF16),
        ),
        in_specs=[SMEM_SPEC] + [VMEM_SPEC] * 8,
        out_specs=(VMEM_SPEC, VMEM_SPEC),
        compiler_params=params(),
        name="project_far",
    )(where, *tokens, far_mine, far_theirs, near, bias)

    partner = swap(keyvals, 1)
    rim = lax.ppermute(
        keyvals[3], "expert", [(i, i + 7) for i in range(size - 8) if i & 1]
    )
    behind = jnp.concatenate([rim[None], partner], axis=0)
    attended = pl.pallas_call(
        attend,
        out_shape=jax.ShapeDtypeStruct((4, rows, QUERY_COLS), BF16),
        in_specs=[SMEM_SPEC] + [VMEM_SPEC] * 3 + [SMEM_SPEC],
        out_specs=VMEM_SPEC,
        compiler_params=params(),
        name="attend",
    )(where, queries, keyvals, behind, attention_sink_logits[0])
    heads = jnp.stack(spread_out([pick(attended, r) for r in range(4)]))

    residual, normed_mid = pl.pallas_call(
        out_project,
        out_shape=(jax.ShapeDtypeStruct((rows, width), BF16),) * 2,
        grid_spec=pltpu.PrefetchScalarGridSpec(
            num_scalar_prefetch=1,
            grid=(4,),
            in_specs=[
                pl.BlockSpec((1, rows, QUERY_COLS), lambda r, where: (r, 0, 0)),
                pl.BlockSpec((QUERY_COLS, width), lambda r, where: (where[1] ^ r, 0)),
                pl.BlockSpec((rows, width), lambda r, where: (0, 0)),
                pl.BlockSpec((1, width), lambda r, where: (0, 0)),
                pl.BlockSpec((1, width), lambda r, where: (0, 0)),
            ],
            out_specs=(pl.BlockSpec((rows, width), lambda r, where: (0, 0)),) * 2,
            scratch_shapes=[pltpu.VMEM((rows, width), F32)],
        ),
        compiler_params=params(),
        name="out_project",
    )(where, heads, out_weight[0], state, out_bias, expert_gain)

    gate_up, down = gate_up_weight[0, 0], down_weight[0, 0]
    tiles = [(gate_up, down), (swap(gate_up, 1), swap(down, 1))]
    reach = jnp.stack([placement[0][half * 4 + (own ^ r)] for r in range(4)])
    hot, weight_own = routing(expert_ids[0], gate_logits[0], reach, slots)
    far_hot, weight_far = routing(swap(expert_ids[0], 8), swap(gate_logits[0], 8), reach, slots)

    far_mid = swap(normed_mid, 8)
    near_rows = spread_out(list(packed(hot, normed_mid)))
    far_rows = spread_out(list(packed(far_hot, far_mid)))
    near_out = expert(jnp.stack(near_rows), tiles)
    far_out = expert(jnp.stack(far_rows), tiles)
    far_sum = unpacked(far_hot, weight_far, jnp.stack(spread_out(list(far_out)))).astype(BF16)
    near_sum = unpacked(hot, weight_own, jnp.stack(spread_out(list(near_out))))
    near_sum = (residual.astype(F32) + near_sum).astype(BF16)

    sections = lax.axis_size("section")
    ahead = [
        (s * size + i, (s + 1) % sections * size + (i ^ 8))
        for s in range(sections)
        for i in range(size)
    ]
    far_sum = lax.ppermute(far_sum, ("section", "expert"), ahead)
    near_sum = lax.ppermute(
        near_sum, "section", [(s, (s + 1) % sections) for s in range(sections)]
    )
    return (near_sum.astype(F32) + far_sum.astype(F32)).astype(BF16)[None]


def solution(mesh):
    return jax.shard_map(
        shards,
        mesh=mesh,
        in_specs=(
            P("section", "expert", None),
            P("section", None),
            P("section", "expert", None),
            P("section", None),
            P("section", None, None),
            P("section", None),
            P("section", None),
            P("section", None),
            P("section", "expert", None, None),
            P("section", "expert", None, None),
            P("section", "expert", None),
            P("section", "expert", None),
            P("section", None),
        ),
        out_specs=P("section", "expert", None),
        check_vma=False,
    )
```

```python
import jax
import jax.numpy as jnp
from jax import lax
from jax.experimental import pallas as pl
from jax.experimental.pallas import tpu as pltpu
from jax.sharding import PartitionSpec as P

HEAD_DIM = 64
QUERY_HEADS = 32
KEY_VALUE_HEADS = 4
WINDOW_TOKENS = 128
TOP = 4
GROUP = QUERY_HEADS // KEY_VALUE_HEADS
QUERY_COLS = GROUP * HEAD_DIM
GROUP_COLS = QUERY_COLS + 2 * HEAD_DIM
BF16 = jnp.bfloat16
F32 = jnp.float32
VMEM_BYTES = 50 * 1024 * 1024


def swap(x, mask):
    size = lax.axis_size("expert")
    return lax.ppermute(x, "expert", [(i, i ^ mask) for i in range(size)])


def normed(vector, gain_row):
    as_float = vector.astype(F32)
    inverse_rms = lax.rsqrt(jnp.mean(as_float * as_float, axis=-1, keepdims=True) + 1e-05)
    return (as_float * inverse_rms * gain_row).astype(BF16)


def params(limit=VMEM_BYTES):
    return pltpu.CompilerParams(vmem_limit_bytes=limit)


SMEM_SPEC = pl.BlockSpec(memory_space=pltpu.SMEM)
VMEM_SPEC = pl.BlockSpec(memory_space=pltpu.VMEM)


def project_rows(base, own, tokens, weights):
    depth = weights.shape[1]
    odd = (own & 1) == 1
    total = None
    for r in (0, 2):
        pair = (weights[r], weights[r + 1])
        ordered = jnp.concatenate(
            [jnp.where(odd, pair[1], pair[0]), jnp.where(odd, pair[0], pair[1])], axis=0
        )
        start = pl.multiple_of((base * 4 + ((own & 2) ^ r)) * depth, 128)
        columns = pl.ds(start, 2 * depth)
        stacked = jnp.concatenate([t[:, columns] for t in tokens], axis=0)
        part = jnp.dot(stacked, ordered, preferred_element_type=F32)
        total = part if total is None else total + part
    return total


def project_near(where, t0, t1, t2, t3, mine, theirs, out):
    half, own, core = where[0], where[1], where[2]
    tokens = (t0, t1, t2, t3)
    out[...] = project_rows(2 * half + core, own, tokens, mine) + project_rows(
        2 * half + 1 - core, own, tokens, theirs
    )


def project_more(where, t0, t1, t2, t3, mine, before, out):
    half, own, core = where[0], where[1], where[2]
    tokens = (t0, t1, t2, t3)
    out[...] = before[...] + project_rows(2 * (1 - half) + core, own, tokens, mine)


def project_last(where, t0, t1, t2, t3, theirs, before, bias, queries, keyvals):
    half, own, core = where[0], where[1], where[2]
    tokens = (t0, t1, t2, t3)
    total = before[...] + project_rows(2 * (1 - half) + 1 - core, own, tokens, theirs)
    rows = t0.shape[0]
    projected = (total + bias[pl.ds(own, 1), :]).astype(BF16)
    for r in range(4):
        block = projected[r * rows : (r + 1) * rows]
        queries[own ^ r] = block[:, :QUERY_COLS]
        keyvals[own ^ r] = block[:, QUERY_COLS:]


def attend(where, queries, keyvals, behind, sinks, out):
    half, own, core = where[0], where[1], where[2]
    rows = queries.shape[1]
    shape = (2 * rows, GROUP * rows)
    key_at = lax.broadcasted_iota(jnp.int32, shape, 0)
    distance = lax.rem(lax.broadcasted_iota(jnp.int32, shape, 1), rows) - key_at + rows
    band = (distance >= 0) & (distance < WINDOW_TOKENS)
    sink = jnp.concatenate(
        [jnp.full((1, rows), sinks[own * GROUP + j], F32) for j in range(GROUP)], axis=1
    )
    for b in range(4):
        both = jnp.concatenate([behind[b + core], keyvals[b]], axis=0)
        turned = queries[b].T
        heads = jnp.concatenate(
            [turned[j * HEAD_DIM : (j + 1) * HEAD_DIM] for j in range(GROUP)], axis=1
        )
        scores = jnp.dot(both[:, :HEAD_DIM], heads, preferred_element_type=F32) * 0.125
        inside = band
        if b == 0:
            first_key = jnp.where((half == 0) & (core == 0), rows, 0)
            inside = band & (key_at >= first_key)
        masked = jnp.where(inside, scores, -1e30)
        peak = jnp.maximum(jnp.max(masked, axis=0, keepdims=True), sink)
        numer = jnp.where(inside, jnp.exp(masked - peak), 0.0)
        denominator = jnp.sum(numer, axis=0, keepdims=True) + jnp.exp(sink - peak)
        weights = (numer / denominator).astype(BF16)
        mixed = lax.dot_general(
            both[:, HEAD_DIM:], weights, (((0,), (0,)), ((), ())), preferred_element_type=F32
        ).astype(BF16)
        out[b] = jnp.concatenate(
            [mixed[:, j * rows : (j + 1) * rows] for j in range(GROUP)], axis=0
        ).T


def routing(ids, logits, experts, slots):
    gates = jax.nn.softmax(logits, axis=-1)
    hits = ids[None, :, :] == experts[:, None, None]
    chosen = jnp.any(hits, axis=-1)
    weight = jnp.sum(jnp.where(hits, gates[None], 0.0), axis=-1)
    rows = ids.shape[0]
    earlier = jnp.arange(rows)[:, None] < jnp.arange(rows)[None, :]
    rank = jnp.dot(chosen.astype(BF16), earlier.astype(BF16), preferred_element_type=F32)
    slot = jnp.arange(slots, dtype=jnp.int32)
    one_hot = (rank.astype(jnp.int32)[:, None, :] == slot[None, :, None]) & chosen[:, None, :]
    return one_hot.astype(BF16), weight


def packed(one_hot, rows):
    return jnp.einsum("rst,td->rsd", one_hot, rows, preferred_element_type=F32).astype(BF16)


def unpacked(one_hot, weight, results):
    spread = jnp.einsum("rst,rsd->rtd", one_hot, results, preferred_element_type=F32)
    return jnp.sum(spread * weight[:, :, None], axis=0)


def swiglu(hidden):
    half_cols = hidden.shape[1] // 2
    gate_part = hidden[:, :half_cols]
    up_part = hidden[:, half_cols:]
    return ((up_part + 1.0) * gate_part * jax.nn.sigmoid(1.702 * gate_part)).astype(BF16)


def joined(parts):
    return jnp.stack(parts).reshape(-1, parts[0].shape[-1])


def activations(pieces, tiles):
    acts = []
    for gate_up, _ in tiles:
        hidden, start = 0.0, 0
        for piece in pieces:
            end = start + piece.shape[-1]
            hidden += jnp.dot(piece, gate_up[start:end], preferred_element_type=F32)
            start = end
        acts.append(swiglu(hidden))
    return lax.optimization_barrier(acts)


def expert_out(acts, tiles, start, end):
    total = 0.0
    for act, (_, down) in zip(acts, tiles):
        part = jnp.dot(act, down[:, start:end], preferred_element_type=F32).astype(BF16)
        total = total + part.astype(F32)
    return list(total.astype(BF16).reshape(4, -1, end - start))


def spread_out(blocks):
    return [blocks[0]] + [swap(blocks[r], 2 * r) for r in range(1, 4)]


def shards(
    section_input,
    attention_gain,
    query_key_value_weight,
    qkv_bias,
    out_weight,
    out_bias,
    attention_sink_logits,
    expert_gain,
    gate_up_weight,
    down_weight,
    expert_ids,
    gate_logits,
    placement,
):
    rows, width = section_input.shape[1:]
    experts_count = placement.shape[1]
    slots = 2 * min(rows // 2, rows * TOP * 5 // (8 * experts_count))
    me = lax.axis_index("expert").astype(jnp.int32)
    half, own, core = me >> 3, (me >> 1) & 3, me & 1
    where = jnp.stack([half, own, core])
    state = section_input[0]

    weight = query_key_value_weight[0]
    weight_rows = weight.shape[0]
    depth = -(-weight_rows // 64) * 64
    query_end = QUERY_HEADS * HEAD_DIM
    key_end = query_end + KEY_VALUE_HEADS * HEAD_DIM

    def grouped(array):
        lead = array.shape[0]
        return jnp.concatenate(
            [
                array[:, :query_end].reshape(lead, 4, QUERY_COLS),
                array[:, query_end:key_end].reshape(lead, 4, HEAD_DIM),
                array[:, key_end:].reshape(lead, 4, HEAD_DIM),
            ],
            axis=2,
        )

    by_group = jnp.pad(grouped(weight).transpose(1, 0, 2), ((0, 0), (0, depth - weight_rows), (0, 0)))
    bias = grouped(qkv_bias)[0]
    pick = lambda array, r: lax.dynamic_index_in_dim(array, own ^ r, 0, keepdims=False)
    gate_up, down = gate_up_weight[0, 0], down_weight[0, 0]
    size = lax.axis_size("expert")
    normed_in = normed(state, attention_gain[0])
    blocked = jnp.pad(
        normed_in.reshape(rows, 2, 4, 2, width // size).transpose(0, 1, 3, 2, 4),
        ((0, 0),) * 4 + ((0, depth - width // size),),
    ).reshape(rows, size * depth)

    by_group_far = swap(by_group, 8)
    across, along = swap(blocked, 2), swap(blocked, 4)
    gate_up_other, down_other = swap(gate_up, 1), swap(down, 1)
    by_group, across, along, gate_up_other, down_other = lax.optimization_barrier(
        (by_group, across, along, gate_up_other, down_other)
    )
    corner = swap(along, 2)
    near_blocks = spread_out([pick(by_group, r) for r in range(4)])
    by_group_far, corner, near_blocks = lax.optimization_barrier(
        (by_group_far, corner, near_blocks)
    )
    tokens = [blocked, across, along, corner]
    near_mine = jnp.stack(near_blocks)
    near_theirs = swap(near_mine, 1)
    far_mine = jnp.stack(spread_out([pick(by_group_far, r) for r in range(4)]))
    far_theirs = swap(far_mine, 1)

    total_shape = jax.ShapeDtypeStruct((4 * rows, GROUP_COLS), F32)
    total = pl.pallas_call(
        project_near,
        out_shape=total_shape,
        in_specs=[SMEM_SPEC] + [VMEM_SPEC] * 6,
        out_specs=VMEM_SPEC,
        compiler_params=params(),
        name="project_near",
    )(where, *tokens, near_mine, near_theirs)
    total = pl.pallas_call(
        project_more,
        out_shape=total_shape,
        in_specs=[SMEM_SPEC] + [VMEM_SPEC] * 6,
        out_specs=VMEM_SPEC,
        compiler_params=params(),
        name="project_more",
    )(where, *tokens, far_mine, total)
    queries, keyvals = pl.pallas_call(
        project_last,
        out_shape=(
            jax.ShapeDtypeStruct((4, rows, QUERY_COLS), BF16),
            jax.ShapeDtypeStruct((4, rows, 2 * HEAD_DIM), BF16),
        ),
        in_specs=[SMEM_SPEC] + [VMEM_SPEC] * 7,
        out_specs=(VMEM_SPEC, VMEM_SPEC),
        compiler_params=params(),
        name="project_last",
    )(where, *tokens, far_theirs, total, bias)

    partner = swap(keyvals, 1)
    rim = lax.ppermute(
        keyvals[3], "expert", [(i, i + 7) for i in range(size - 8) if i & 1]
    )
    behind = jnp.concatenate([rim[None], partner], axis=0)
    attended = pl.pallas_call(
        attend,
        out_shape=jax.ShapeDtypeStruct((4, rows, QUERY_COLS), BF16),
        in_specs=[SMEM_SPEC] + [VMEM_SPEC] * 3 + [SMEM_SPEC],
        out_specs=VMEM_SPEC,
        compiler_params=params(),
        name="attend",
    )(where, queries, keyvals, behind, attention_sink_logits[0])
    heads = spread_out([pick(attended, r) for r in range(4)])
    by_head = jnp.zeros((rows, QUERY_HEADS * HEAD_DIM), BF16)
    for r in range(4):
        by_head = lax.dynamic_update_slice(by_head, heads[r], (0, (own ^ r) * QUERY_COLS))
    residual = (
        state.astype(F32)
        + jnp.dot(by_head, out_weight[0], preferred_element_type=F32)
        + out_bias[0]
    ).astype(BF16)
    normed_mid = normed(residual, expert_gain[0])

    tiles = [(gate_up, down), (gate_up_other, down_other)]
    reach = jnp.stack([placement[0][half * 4 + (own ^ r)] for r in range(4)])
    ids, logits = expert_ids[0], gate_logits[0]
    far_choice = swap(jnp.concatenate([ids.astype(F32), logits], axis=1), 8)
    hot, weight_own = routing(ids, logits, reach, slots)
    far_hot, weight_far = routing(
        far_choice[:, :TOP].astype(jnp.int32), far_choice[:, TOP:], reach, slots
    )

    cut = (width // 256 + 1) * 128
    spans = [(0, cut), (cut, width)]
    far_mid = [swap(normed_mid[:, a:b], 8) for a, b in spans]
    near_rows = spread_out(list(packed(hot, normed_mid)))
    far_rows = [spread_out(list(packed(far_hot, mid))) for mid in far_mid]
    near_out = expert_out(activations([joined(near_rows)], tiles), tiles, 0, width)
    far_rows, near_out = lax.optimization_barrier((far_rows, near_out))
    far_acts = activations([joined(rows_in) for rows_in in far_rows], tiles)
    far_back = [spread_out(expert_out(far_acts, tiles, a, b)) for a, b in spans]
    far_sum = [
        unpacked(far_hot, weight_far, jnp.stack(back)).astype(BF16) for back in far_back
    ]

    sections = lax.axis_size("section")
    ahead = [
        (s * size + i, (s + 1) % sections * size + (i ^ 8))
        for s in range(sections)
        for i in range(size)
    ]
    far_sum = [lax.ppermute(part, ("section", "expert"), ahead) for part in far_sum]
    near_sum = unpacked(hot, weight_own, jnp.stack(spread_out(near_out)))
    near_sum = (residual.astype(F32) + near_sum).astype(BF16)
    near_sum = lax.ppermute(
        near_sum, "section", [(s, (s + 1) % sections) for s in range(sections)]
    )
    far_sum = jnp.concatenate(far_sum, axis=1)
    return (near_sum.astype(F32) + far_sum.astype(F32)).astype(BF16)[None]


def solution(mesh):
    return jax.shard_map(
        shards,
        mesh=mesh,
        in_specs=(
            P("section", "expert", None),
            P("section", None),
            P("section", "expert", None),
            P("section", None),
            P("section", None, None),
            P("section", None),
            P("section", None),
            P("section", None),
            P("section", "expert", None, None),
            P("section", "expert", None, None),
            P("section", "expert", None),
            P("section", "expert", None),
            P("section", None),
        ),
        out_specs=P("section", "expert", None),
        check_vma=False,
    )
```

```python
import functools

import jax
import jax.numpy as jnp
from jax import lax
from jax.experimental import pallas as pl
from jax.experimental.pallas import tpu as pltpu
from jax.sharding import PartitionSpec as P

HEAD_DIM = 64
QUERY_HEADS = 32
KEY_VALUE_HEADS = 4
WINDOW_TOKENS = 128
TOP = 4
GROUP = QUERY_HEADS // KEY_VALUE_HEADS
QUERY_COLS = GROUP * HEAD_DIM
GROUP_COLS = QUERY_COLS + 2 * HEAD_DIM
BF16 = jnp.bfloat16
F32 = jnp.float32
VMEM_BYTES = 50 * 1024 * 1024


def swap(x, mask):
    size = lax.axis_size("expert")
    return lax.ppermute(x, "expert", [(i, i ^ mask) for i in range(size)])


def normed(vector, gain_row):
    as_float = vector.astype(F32)
    inverse_rms = lax.rsqrt(jnp.mean(as_float * as_float, axis=-1, keepdims=True) + 1e-05)
    return (as_float * inverse_rms * gain_row).astype(BF16)


def params(limit=VMEM_BYTES):
    return pltpu.CompilerParams(vmem_limit_bytes=limit)


SMEM_SPEC = pl.BlockSpec(memory_space=pltpu.SMEM)
VMEM_SPEC = pl.BlockSpec(memory_space=pltpu.VMEM)


def regroup(where, weight, *blocks):
    own = where[1]
    query_end = QUERY_HEADS * HEAD_DIM
    for r in range(4):
        group = own ^ r
        odd = (group & 1) == 1
        queries = weight[:, pl.ds(pl.multiple_of(group * QUERY_COLS, 128), QUERY_COLS)]
        halves = []
        for start in (query_end, query_end + KEY_VALUE_HEADS * HEAD_DIM):
            at = pl.multiple_of(start + (group >> 1) * 2 * HEAD_DIM, 128)
            pair = weight[:, pl.ds(at, 2 * HEAD_DIM)]
            halves.append(jnp.where(odd, pair[:, HEAD_DIM:], pair[:, :HEAD_DIM]))
        blocks[r][:, :QUERY_COLS] = queries
        blocks[r][:, QUERY_COLS:] = jnp.concatenate(halves, axis=1)


def project_rows(base, own, tokens, weights):
    depth = weights.shape[1]
    odd = (own & 1) == 1
    total = None
    for r in (0, 2):
        pair = (weights[r], weights[r + 1])
        ordered = jnp.concatenate(
            [jnp.where(odd, pair[1], pair[0]), jnp.where(odd, pair[0], pair[1])], axis=0
        )
        start = pl.multiple_of((base * 4 + ((own & 2) ^ r)) * depth, 128)
        columns = pl.ds(start, 2 * depth)
        stacked = jnp.concatenate([t[:, columns] for t in tokens], axis=0)
        part = jnp.dot(stacked, ordered, preferred_element_type=F32)
        total = part if total is None else total + part
    return total


def project_near(where, t0, t1, t2, t3, mine, theirs, out):
    half, own, core = where[0], where[1], where[2]
    tokens = (t0, t1, t2, t3)
    out[...] = project_rows(2 * half + core, own, tokens, mine) + project_rows(
        2 * half + 1 - core, own, tokens, theirs
    )


def project_more(where, t0, t1, t2, t3, mine, before, out):
    half, own, core = where[0], where[1], where[2]
    tokens = (t0, t1, t2, t3)
    out[...] = before[...] + project_rows(2 * (1 - half) + core, own, tokens, mine)


def project_last(where, t0, t1, t2, t3, theirs, before, bias, queries, keyvals):
    half, own, core = where[0], where[1], where[2]
    tokens = (t0, t1, t2, t3)
    total = before[...] + project_rows(2 * (1 - half) + 1 - core, own, tokens, theirs)
    rows = t0.shape[0]
    projected = (total + bias[pl.ds(own, 1), :]).astype(BF16)
    for r in range(4):
        block = projected[r * rows : (r + 1) * rows]
        queries[own ^ r] = block[:, :QUERY_COLS]
        keyvals[own ^ r] = block[:, QUERY_COLS:]


def attend(where, queries, keyvals, behind, sinks, out):
    half, own, core = where[0], where[1], where[2]
    rows = queries.shape[1]
    shape = (2 * rows, GROUP * rows)
    key_at = lax.broadcasted_iota(jnp.int32, shape, 0)
    distance = lax.rem(lax.broadcasted_iota(jnp.int32, shape, 1), rows) - key_at + rows
    band = (distance >= 0) & (distance < WINDOW_TOKENS)
    sink = jnp.concatenate(
        [jnp.full((1, rows), sinks[own * GROUP + j], F32) for j in range(GROUP)], axis=1
    )
    for b in range(4):
        both = jnp.concatenate([behind[b + core], keyvals[b]], axis=0)
        turned = queries[b].T
        heads = jnp.concatenate(
            [turned[j * HEAD_DIM : (j + 1) * HEAD_DIM] for j in range(GROUP)], axis=1
        )
        scores = jnp.dot(both[:, :HEAD_DIM], heads, preferred_element_type=F32) * 0.125
        inside = band
        if b == 0:
            first_key = jnp.where((half == 0) & (core == 0), rows, 0)
            inside = band & (key_at >= first_key)
        masked = jnp.where(inside, scores, -1e30)
        peak = jnp.maximum(jnp.max(masked, axis=0, keepdims=True), sink)
        numer = jnp.where(inside, jnp.exp(masked - peak), 0.0)
        denominator = jnp.sum(numer, axis=0, keepdims=True) + jnp.exp(sink - peak)
        weights = (numer / denominator).astype(BF16)
        mixed = lax.dot_general(
            both[:, HEAD_DIM:], weights, (((0,), (0,)), ((), ())), preferred_element_type=F32
        ).astype(BF16)
        out[b] = jnp.concatenate(
            [mixed[:, j * rows : (j + 1) * rows] for j in range(GROUP)], axis=0
        ).T


def routing(ids, logits, experts, slots):
    gates = jax.nn.softmax(logits, axis=-1)
    hits = ids[None, :, :] == experts[:, None, None]
    chosen = jnp.any(hits, axis=-1)
    weight = jnp.sum(jnp.where(hits, gates[None], 0.0), axis=-1)
    rows = ids.shape[0]
    earlier = jnp.arange(rows)[:, None] < jnp.arange(rows)[None, :]
    rank = jnp.dot(chosen.astype(BF16), earlier.astype(BF16), preferred_element_type=F32)
    slot = jnp.arange(slots, dtype=jnp.int32)
    one_hot = (rank.astype(jnp.int32)[:, None, :] == slot[None, :, None]) & chosen[:, None, :]
    return one_hot.astype(BF16), weight


def packed(one_hot, rows):
    return jnp.einsum("rst,td->rsd", one_hot, rows, preferred_element_type=F32).astype(BF16)


def unpacked(one_hot, weight, results):
    spread = jnp.einsum("rst,rsd->rtd", one_hot, results, preferred_element_type=F32)
    return jnp.sum(spread * weight[:, :, None], axis=0)


def turn_kernel(source, out):
    hid, room = source.shape[0] // 2, out.shape[1] // 2
    empty = jnp.zeros((out.shape[0], room - hid), out.dtype)
    out[:, :room] = jnp.concatenate([source[:hid].T, empty], axis=1)
    out[:, room:] = jnp.concatenate([source[hid:].T, empty], axis=1)


def turned(array):
    lines, width = array.shape
    room = 2 * -(-lines // 256) * 128
    step = 640
    return pl.pallas_call(
        turn_kernel,
        out_shape=jax.ShapeDtypeStruct((width, room), array.dtype),
        grid=(-(-width // step),),
        in_specs=[pl.BlockSpec((lines, step), lambda i: (0, i))],
        out_specs=pl.BlockSpec((step, room), lambda i: (i, 0)),
        compiler_params=params(),
        name="turned",
    )(array)


DEPTH_CHUNK = 640


def expert_kernel(count, *refs):
    blocks, sources = refs[:count], refs[count : count + 4]
    outs, (gate_up, down, total, sems) = refs[count + 4 : -4], refs[-4:]
    width, both = gate_up.shape[1:]
    room, hid = both // 2, down.shape[1]
    starts = list(range(0, width, DEPTH_CHUNK))
    up_copies, down_copies = [], []
    for tile in range(2):
        up_copies.append(
            [
                pltpu.make_async_copy(
                    sources[2 * tile].at[pl.ds(at, min(DEPTH_CHUNK, width - at))],
                    gate_up.at[tile, pl.ds(at, min(DEPTH_CHUNK, width - at))],
                    sems.at[tile, n],
                )
                for n, at in enumerate(starts)
            ]
        )
        down_copies.append(
            pltpu.make_async_copy(
                sources[2 * tile + 1], down.at[tile], sems.at[tile, len(starts)]
            )
        )
    for tile in range(2):
        for copy in up_copies[tile]:
            copy.start()
        down_copies[tile].start()
    rows = jnp.concatenate([block[...] for block in blocks], axis=0)
    for tile in range(2):
        hidden = None
        for copy, at in zip(up_copies[tile], starts):
            copy.wait()
            end = min(at + DEPTH_CHUNK, width)
            part = jnp.dot(rows[:, at:end], gate_up[tile, at:end], preferred_element_type=F32)
            hidden = part if hidden is None else hidden + part
        gate, up = hidden[:, :room], hidden[:, room:]
        act = ((up + 1.0) * gate * jax.nn.sigmoid(1.702 * gate)).astype(BF16)
        down_copies[tile].wait()
        part = jnp.dot(act[:, :hid], down[tile], preferred_element_type=F32).astype(BF16)
        if tile == 0:
            total[...] = part
    summed = (total[...].astype(F32) + part.astype(F32)).astype(BF16)
    slots = blocks[0].shape[0]
    for n, out in enumerate(outs):
        out[...] = summed[n * slots : (n + 1) * slots]


def expert(blocks, tiles, name):
    count = len(blocks)
    slots, width = blocks[0].shape
    hid = tiles[0][1].shape[0]
    any_spec = pl.BlockSpec(memory_space=pl.ANY)
    return pl.pallas_call(
        functools.partial(expert_kernel, count),
        out_shape=(jax.ShapeDtypeStruct((slots, width), BF16),) * count,
        in_specs=[VMEM_SPEC] * count + [any_spec] * 4,
        out_specs=(VMEM_SPEC,) * count,
        scratch_shapes=[
            pltpu.VMEM((2, width, tiles[0][0].shape[1]), BF16),
            pltpu.VMEM((2, hid, width), BF16),
            pltpu.VMEM((count * slots, width), BF16),
            pltpu.SemaphoreType.DMA((2, -(-width // DEPTH_CHUNK) + 1)),
        ],
        compiler_params=params(),
        cost_estimate=pl.CostEstimate(
            flops=2 * 2 * count * slots * width * 3 * hid,
            bytes_accessed=2 * 2 * 3 * hid * width + 4 * count * slots * width,
            transcendentals=2 * count * slots * hid,
        ),
        name=name,
    )(*blocks, *tiles[0], *tiles[1])


def spread_out(blocks):
    return [blocks[0]] + [swap(blocks[r], 2 * r) for r in range(1, 4)]


def shards(
    section_input,
    attention_gain,
    query_key_value_weight,
    qkv_bias,
    out_weight,
    out_bias,
    attention_sink_logits,
    expert_gain,
    gate_up_weight,
    down_weight,
    expert_ids,
    gate_logits,
    placement,
):
    rows, width = section_input.shape[1:]
    experts_count = placement.shape[1]
    slots = 2 * min(rows // 2, rows * TOP * 5 // (8 * experts_count))
    me = lax.axis_index("expert").astype(jnp.int32)
    half, own, core = me >> 3, (me >> 1) & 3, me & 1
    where = jnp.stack([half, own, core])
    state = section_input[0]

    weight = query_key_value_weight[0]
    weight_rows = weight.shape[0]
    depth = -(-weight_rows // 64) * 64
    query_end = QUERY_HEADS * HEAD_DIM
    key_end = query_end + KEY_VALUE_HEADS * HEAD_DIM

    def grouped(array):
        lead = array.shape[0]
        return jnp.concatenate(
            [
                array[:, :query_end].reshape(lead, 4, QUERY_COLS),
                array[:, query_end:key_end].reshape(lead, 4, HEAD_DIM),
                array[:, key_end:].reshape(lead, 4, HEAD_DIM),
            ],
            axis=2,
        )

    bias = grouped(qkv_bias)[0]
    pick = lambda array, r: lax.dynamic_index_in_dim(array, own ^ r, 0, keepdims=False)
    down = down_weight[0, 0]

    def by_group(rows_in):
        padded = jnp.pad(rows_in, ((0, depth - weight_rows), (0, 0)))
        return pl.pallas_call(
            regroup,
            out_shape=(jax.ShapeDtypeStruct((depth, GROUP_COLS), BF16),) * 4,
            in_specs=[SMEM_SPEC, VMEM_SPEC],
            out_specs=(VMEM_SPEC,) * 4,
            compiler_params=params(),
            name="regroup",
        )(where, padded)

    size = lax.axis_size("expert")
    def columns_of(tokens):
        split = normed(tokens, attention_gain[0]).reshape(rows, 2, 4, 2, width // size)
        return jnp.pad(
            split.transpose(0, 1, 3, 2, 4), ((0, 0),) * 4 + ((0, depth - width // size),)
        ).reshape(rows, size * depth)

    first_rows = depth // 2
    far_first, rest = swap(weight[:first_rows], 8), weight[first_rows:]
    across, along = swap(state, 2), swap(state, 4)
    near_blocks = list(by_group(weight))
    near_blocks[1], near_blocks[3] = swap(near_blocks[1], 2), swap(near_blocks[3], 6)
    gate_up = turned(gate_up_weight[0, 0].T)
    tokens = [columns_of(state)]
    ids, logits = expert_ids[0], gate_logits[0]
    choice = jnp.concatenate([ids.astype(F32), logits], axis=1)
    pairs = half * 4 + (own ^ jnp.arange(4, dtype=jnp.int32))
    at_pair = pairs[:, None] == jnp.arange(experts_count, dtype=jnp.int32)[None, :]
    reach = jnp.sum(jnp.where(at_pair, placement, 0), axis=1)
    hot, gates_own = routing(ids, logits, reach, slots)
    near_blocks, far_first, rest, across, along, gate_up, down, tokens, hot, gates_own, choice = (
        lax.optimization_barrier(
            (near_blocks, far_first, rest, across, along)
            + (gate_up, down, tokens, hot, gates_own, choice)
        )
    )
    weight_far = jnp.concatenate([far_first, swap(rest, 8)], axis=0)
    corner = swap(along, 2)
    near_blocks[2] = swap(near_blocks[2], 4)
    gate_up_other, down_other = swap(gate_up, 1), swap(down, 1)
    tokens += [columns_of(across), columns_of(along)]
    near_blocks, weight_far, corner, tokens, choice = lax.optimization_barrier(
        (near_blocks, weight_far, corner, tokens, choice)
    )
    near_mine = jnp.stack(near_blocks)
    near_theirs = swap(near_mine, 1)
    far_blocks = spread_out(by_group(weight_far))
    far_choice = swap(choice, 8)
    tokens += [columns_of(corner)]

    total_shape = jax.ShapeDtypeStruct((4 * rows, GROUP_COLS), F32)
    total = pl.pallas_call(
        project_near,
        out_shape=total_shape,
        in_specs=[SMEM_SPEC] + [VMEM_SPEC] * 6,
        out_specs=VMEM_SPEC,
        compiler_params=params(),
        name="project_near",
    )(where, *tokens, near_mine, near_theirs)
    total, far_blocks, far_choice = lax.optimization_barrier((total, far_blocks, far_choice))
    far_mine = jnp.stack(far_blocks)
    far_theirs = swap(far_mine, 1)
    total = pl.pallas_call(
        project_more,
        out_shape=total_shape,
        in_specs=[SMEM_SPEC] + [VMEM_SPEC] * 6,
        out_specs=VMEM_SPEC,
        compiler_params=params(),
        name="project_more",
    )(where, *tokens, far_mine, total)
    queries, keyvals = pl.pallas_call(
        project_last,
        out_shape=(
            jax.ShapeDtypeStruct((4, rows, QUERY_COLS), BF16),
            jax.ShapeDtypeStruct((4, rows, 2 * HEAD_DIM), BF16),
        ),
        in_specs=[SMEM_SPEC] + [VMEM_SPEC] * 7,
        out_specs=(VMEM_SPEC, VMEM_SPEC),
        compiler_params=params(),
        name="project_last",
    )(where, *tokens, far_theirs, total, bias)

    partner = swap(keyvals, 1)
    rim = lax.ppermute(
        keyvals[3], "expert", [(i, i + 7) for i in range(size - 8) if i & 1]
    )
    behind = jnp.concatenate([rim[None], partner], axis=0)
    attended = pl.pallas_call(
        attend,
        out_shape=jax.ShapeDtypeStruct((4, rows, QUERY_COLS), BF16),
        in_specs=[SMEM_SPEC] + [VMEM_SPEC] * 3 + [SMEM_SPEC],
        out_specs=VMEM_SPEC,
        compiler_params=params(),
        name="attend",
    )(where, queries, keyvals, behind, attention_sink_logits[0])
    heads = spread_out([pick(attended, r) for r in range(4)])
    far_hot, gates_far = routing(
        far_choice[:, :TOP].astype(jnp.int32), far_choice[:, TOP:], reach, slots
    )
    heads, far_hot, gates_far = lax.optimization_barrier((heads, far_hot, gates_far))
    by_head = jnp.zeros((rows, QUERY_HEADS * HEAD_DIM), BF16)
    for r in range(4):
        by_head = lax.dynamic_update_slice(by_head, heads[r], (0, (own ^ r) * QUERY_COLS))
    residual = (
        state.astype(F32)
        + jnp.dot(by_head, out_weight[0], preferred_element_type=F32)
        + out_bias[0]
    ).astype(BF16)
    normed_mid = normed(residual, expert_gain[0])
    normed_mid, gate_up_other, down_other = lax.optimization_barrier(
        (normed_mid, gate_up_other, down_other)
    )

    tiles = [(gate_up, down), (gate_up_other, down_other)]
    far_mid = swap(normed_mid, 8)
    near_rows = spread_out(list(packed(hot, normed_mid)))
    far_rows = spread_out(list(packed(far_hot, far_mid)))
    early = expert(near_rows + far_rows[:1], tiles, "near_expert")
    far_rows, early = lax.optimization_barrier((far_rows, early))
    near_out = early[:4]
    far_out = early[4:] + expert(far_rows[1:], tiles, "far_expert")
    far_sum = unpacked(far_hot, gates_far, jnp.stack(spread_out(far_out))).astype(BF16)

    sections = lax.axis_size("section")
    ahead = [
        (s * size + i, (s + 1) % sections * size + (i ^ 8))
        for s in range(sections)
        for i in range(size)
    ]
    far_sum = lax.ppermute(far_sum, ("section", "expert"), ahead)
    near_sum = unpacked(hot, gates_own, jnp.stack(spread_out(near_out)))
    near_sum = (residual.astype(F32) + near_sum).astype(BF16)
    near_sum = lax.ppermute(
        near_sum, "section", [(s, (s + 1) % sections) for s in range(sections)]
    )
    return (near_sum.astype(F32) + far_sum.astype(F32)).astype(BF16)[None]


def solution(mesh):
    return jax.shard_map(
        shards,
        mesh=mesh,
        in_specs=(
            P("section", "expert", None),
            P("section", None),
            P("section", "expert", None),
            P("section", None),
            P("section", None, None),
            P("section", None),
            P("section", None),
            P("section", None),
            P("section", "expert", None, None),
            P("section", "expert", None, None),
            P("section", "expert", None),
            P("section", "expert", None),
            P("section", None),
        ),
        out_specs=P("section", "expert", None),
        check_vma=False,
    )
```

```python
import functools

import jax
import jax.numpy as jnp
from jax import lax
from jax.experimental import pallas as pl
from jax.experimental.pallas import tpu as pltpu
from jax.sharding import PartitionSpec as P

HEAD_DIM = 64
QUERY_HEADS = 32
KEY_VALUE_HEADS = 4
WINDOW_TOKENS = 128
TOP = 4
GROUP = QUERY_HEADS // KEY_VALUE_HEADS
QUERY_COLS = GROUP * HEAD_DIM
GROUP_COLS = QUERY_COLS + 2 * HEAD_DIM
BF16 = jnp.bfloat16
F32 = jnp.float32
VMEM_BYTES = 50 * 1024 * 1024


def swap(x, mask):
    size = lax.axis_size("expert")
    return lax.ppermute(x, "expert", [(i, i ^ mask) for i in range(size)])


def normed(vector, gain_row):
    as_float = vector.astype(F32)
    inverse_rms = lax.rsqrt(jnp.mean(as_float * as_float, axis=-1, keepdims=True) + 1e-05)
    return (as_float * inverse_rms * gain_row).astype(BF16)


def params(limit=VMEM_BYTES):
    return pltpu.CompilerParams(vmem_limit_bytes=limit)


SMEM_SPEC = pl.BlockSpec(memory_space=pltpu.SMEM)
VMEM_SPEC = pl.BlockSpec(memory_space=pltpu.VMEM)


def regroup(where, upper, lower, *blocks):
    own = where[1]
    query_end = QUERY_HEADS * HEAD_DIM
    middle = upper.shape[0]
    for part, lines in ((upper, pl.ds(0, middle)), (lower, pl.ds(middle, lower.shape[0]))):
        for r in range(4):
            group = own ^ r
            odd = (group & 1) == 1
            queries = part[:, pl.ds(pl.multiple_of(group * QUERY_COLS, 128), QUERY_COLS)]
            halves = []
            for start in (query_end, query_end + KEY_VALUE_HEADS * HEAD_DIM):
                at = pl.multiple_of(start + (group >> 1) * 2 * HEAD_DIM, 128)
                pair = part[:, pl.ds(at, 2 * HEAD_DIM)]
                halves.append(jnp.where(odd, pair[:, HEAD_DIM:], pair[:, :HEAD_DIM]))
            blocks[r][lines, :QUERY_COLS] = queries
            blocks[r][lines, QUERY_COLS:] = jnp.concatenate(halves, axis=1)


def project_rows(base, own, tokens, weights):
    depth = weights.shape[1]
    odd = (own & 1) == 1
    total = None
    for r in (0, 2):
        pair = (weights[r], weights[r + 1])
        ordered = jnp.concatenate(
            [jnp.where(odd, pair[1], pair[0]), jnp.where(odd, pair[0], pair[1])], axis=0
        )
        start = pl.multiple_of((base * 4 + ((own & 2) ^ r)) * depth, 128)
        columns = pl.ds(start, 2 * depth)
        stacked = jnp.concatenate([t[:, columns] for t in tokens], axis=0)
        part = jnp.dot(stacked, ordered, preferred_element_type=F32)
        total = part if total is None else total + part
    return total


def project_near(where, t0, t1, t2, t3, mine, theirs, out):
    half, own, core = where[0], where[1], where[2]
    tokens = (t0, t1, t2, t3)
    out[...] = project_rows(2 * half + core, own, tokens, mine) + project_rows(
        2 * half + 1 - core, own, tokens, theirs
    )


def project_more(where, t0, t1, t2, t3, mine, before, out):
    half, own, core = where[0], where[1], where[2]
    tokens = (t0, t1, t2, t3)
    out[...] = before[...] + project_rows(2 * (1 - half) + core, own, tokens, mine)


def project_last(where, t0, t1, t2, t3, theirs, before, bias, queries, keyvals):
    half, own, core = where[0], where[1], where[2]
    tokens = (t0, t1, t2, t3)
    total = before[...] + project_rows(2 * (1 - half) + 1 - core, own, tokens, theirs)
    rows = t0.shape[0]
    projected = (total + bias[pl.ds(own, 1), :]).astype(BF16)
    for r in range(4):
        block = projected[r * rows : (r + 1) * rows]
        queries[own ^ r] = block[:, :QUERY_COLS]
        keyvals[own ^ r] = block[:, QUERY_COLS:]


def attend(where, queries, keyvals, behind, sinks, out):
    half, own, core = where[0], where[1], where[2]
    rows = queries.shape[1]
    shape = (2 * rows, GROUP * rows)
    key_at = lax.broadcasted_iota(jnp.int32, shape, 0)
    distance = lax.rem(lax.broadcasted_iota(jnp.int32, shape, 1), rows) - key_at + rows
    band = (distance >= 0) & (distance < WINDOW_TOKENS)
    sink = jnp.concatenate(
        [jnp.full((1, rows), sinks[own * GROUP + j], F32) for j in range(GROUP)], axis=1
    )
    for b in range(4):
        both = jnp.concatenate([behind[b + core], keyvals[b]], axis=0)
        turned = queries[b].T
        heads = jnp.concatenate(
            [turned[j * HEAD_DIM : (j + 1) * HEAD_DIM] for j in range(GROUP)], axis=1
        )
        scores = jnp.dot(both[:, :HEAD_DIM], heads, preferred_element_type=F32) * 0.125
        inside = band
        if b == 0:
            first_key = jnp.where((half == 0) & (core == 0), rows, 0)
            inside = band & (key_at >= first_key)
        masked = jnp.where(inside, scores, -1e30)
        peak = jnp.maximum(jnp.max(masked, axis=0, keepdims=True), sink)
        numer = jnp.where(inside, jnp.exp(masked - peak), 0.0)
        denominator = jnp.sum(numer, axis=0, keepdims=True) + jnp.exp(sink - peak)
        weights = (numer / denominator).astype(BF16)
        mixed = lax.dot_general(
            both[:, HEAD_DIM:], weights, (((0,), (0,)), ((), ())), preferred_element_type=F32
        ).astype(BF16)
        out[b] = jnp.concatenate(
            [mixed[:, j * rows : (j + 1) * rows] for j in range(GROUP)], axis=0
        ).T


def routing(ids, logits, experts, slots):
    gates = jax.nn.softmax(logits, axis=-1)
    hits = ids[None, :, :] == experts[:, None, None]
    chosen = jnp.any(hits, axis=-1)
    weight = jnp.sum(jnp.where(hits, gates[None], 0.0), axis=-1)
    rows = ids.shape[0]
    earlier = jnp.arange(rows)[:, None] < jnp.arange(rows)[None, :]
    rank = jnp.dot(chosen.astype(BF16), earlier.astype(BF16), preferred_element_type=F32)
    slot = jnp.arange(slots, dtype=jnp.int32)
    one_hot = (rank.astype(jnp.int32)[:, None, :] == slot[None, :, None]) & chosen[:, None, :]
    return one_hot.astype(BF16), weight


def packed(one_hot, rows):
    return jnp.einsum("rst,td->rsd", one_hot, rows, preferred_element_type=F32).astype(BF16)


def unpacked(one_hot, weight, results):
    spread = jnp.einsum("rst,rsd->rtd", one_hot, results, preferred_element_type=F32)
    return jnp.sum(spread * weight[:, :, None], axis=0)


def turn_kernel(source, out):
    hid, room = source.shape[0] // 2, out.shape[1] // 2
    empty = jnp.zeros((out.shape[0], room - hid), out.dtype)
    out[:, :room] = jnp.concatenate([source[:hid].T, empty], axis=1)
    out[:, room:] = jnp.concatenate([source[hid:].T, empty], axis=1)


def turned(array):
    lines, width = array.shape
    room = 2 * -(-lines // 256) * 128
    step = 640
    return pl.pallas_call(
        turn_kernel,
        out_shape=jax.ShapeDtypeStruct((width, room), array.dtype),
        grid=(-(-width // step),),
        in_specs=[pl.BlockSpec((lines, step), lambda i: (0, i))],
        out_specs=pl.BlockSpec((step, room), lambda i: (i, 0)),
        compiler_params=params(),
        name="turned",
    )(array)


DEPTH_CHUNK = 1536


def expert_kernel(count, spans, *refs):
    blocks, sources = refs[:count], refs[count : count + 4]
    outs, (gate_up, down, total, sems) = refs[count + 4 : -4], refs[-4:]
    width, both = gate_up.shape[1:]
    room, hid = both // 2, down.shape[1]
    starts = list(range(0, width, DEPTH_CHUNK))
    up_copies, down_copies = [], []
    for tile in range(2):
        up_copies.append(
            [
                pltpu.make_async_copy(
                    sources[2 * tile].at[pl.ds(at, min(DEPTH_CHUNK, width - at))],
                    gate_up.at[tile, pl.ds(at, min(DEPTH_CHUNK, width - at))],
                    sems.at[tile, n],
                )
                for n, at in enumerate(starts)
            ]
        )
        down_copies.append(
            pltpu.make_async_copy(
                sources[2 * tile + 1], down.at[tile], sems.at[tile, len(starts)]
            )
        )
    for tile in range(2):
        for copy in up_copies[tile]:
            copy.start()
        down_copies[tile].start()
    rows = jnp.concatenate([block[...] for block in blocks], axis=0)
    for tile in range(2):
        hidden = None
        for copy, at in zip(up_copies[tile], starts):
            copy.wait()
            end = min(at + DEPTH_CHUNK, width)
            part = jnp.dot(rows[:, at:end], gate_up[tile, at:end], preferred_element_type=F32)
            hidden = part if hidden is None else hidden + part
        gate, up = hidden[:, :room], hidden[:, room:]
        act = ((up + 1.0) * gate * jax.nn.sigmoid(1.702 * gate)).astype(BF16)
        down_copies[tile].wait()
        part = jnp.dot(act[:, :hid], down[tile], preferred_element_type=F32).astype(BF16)
        if tile == 0:
            total[...] = part
    summed = (total[...].astype(F32) + part.astype(F32)).astype(BF16)
    slots = blocks[0].shape[0]
    for n, out in enumerate(outs):
        block, (start, end) = n % count, spans[n // count]
        out[...] = summed[block * slots : (block + 1) * slots, start:end]


def expert(blocks, tiles, spans, name):
    count = len(blocks)
    slots, width = blocks[0].shape
    hid = tiles[0][1].shape[0]
    any_spec = pl.BlockSpec(memory_space=pl.ANY)
    outs = pl.pallas_call(
        functools.partial(expert_kernel, count, spans),
        out_shape=[
            jax.ShapeDtypeStruct((slots, end - start), BF16)
            for start, end in spans
            for _ in blocks
        ],
        in_specs=[VMEM_SPEC] * count + [any_spec] * 4,
        out_specs=[VMEM_SPEC] * (count * len(spans)),
        scratch_shapes=[
            pltpu.VMEM((2, width, tiles[0][0].shape[1]), BF16),
            pltpu.VMEM((2, hid, width), BF16),
            pltpu.VMEM((count * slots, width), BF16),
            pltpu.SemaphoreType.DMA((2, -(-width // DEPTH_CHUNK) + 1)),
        ],
        compiler_params=params(),
        cost_estimate=pl.CostEstimate(
            flops=2 * 2 * count * slots * width * 3 * hid,
            bytes_accessed=2 * 2 * 3 * hid * width + 4 * count * slots * width,
            transcendentals=2 * count * slots * hid,
        ),
        name=name,
    )(*blocks, *tiles[0], *tiles[1])
    return [list(outs[n * count : (n + 1) * count]) for n in range(len(spans))]


def spread_out(blocks):
    return [blocks[0]] + [swap(blocks[r], 2 * r) for r in range(1, 4)]


def shards(
    section_input,
    attention_gain,
    query_key_value_weight,
    qkv_bias,
    out_weight,
    out_bias,
    attention_sink_logits,
    expert_gain,
    gate_up_weight,
    down_weight,
    expert_ids,
    gate_logits,
    placement,
):
    rows, width = section_input.shape[1:]
    experts_count = placement.shape[1]
    slots = 2 * min(rows // 2, rows * TOP * 5 // (8 * experts_count))
    me = lax.axis_index("expert").astype(jnp.int32)
    half, own, core = me >> 3, (me >> 1) & 3, me & 1
    where = jnp.stack([half, own, core])
    state = section_input[0]

    weight = query_key_value_weight[0]
    weight_rows = weight.shape[0]
    depth = -(-weight_rows // 64) * 64
    query_end = QUERY_HEADS * HEAD_DIM
    key_end = query_end + KEY_VALUE_HEADS * HEAD_DIM

    def grouped(array):
        lead = array.shape[0]
        return jnp.concatenate(
            [
                array[:, :query_end].reshape(lead, 4, QUERY_COLS),
                array[:, query_end:key_end].reshape(lead, 4, HEAD_DIM),
                array[:, key_end:].reshape(lead, 4, HEAD_DIM),
            ],
            axis=2,
        )

    bias = grouped(qkv_bias)[0]
    pick = lambda array, r: lax.dynamic_index_in_dim(array, own ^ r, 0, keepdims=False)
    down = down_weight[0, 0]

    size = lax.axis_size("expert")
    first_rows = depth // 32 * 16 + 16
    upper = weight[:first_rows]
    lower = jnp.pad(weight[first_rows:], ((0, depth - weight_rows), (0, 0)))

    def by_group(upper, lower):
        return pl.pallas_call(
            regroup,
            out_shape=(jax.ShapeDtypeStruct((depth, GROUP_COLS), BF16),) * 4,
            in_specs=[SMEM_SPEC, VMEM_SPEC, VMEM_SPEC],
            out_specs=(VMEM_SPEC,) * 4,
            compiler_params=params(),
            name="regroup",
        )(where, upper, lower)

    def columns_of(tokens):
        split = normed(tokens, attention_gain[0]).reshape(rows, 2, 4, 2, width // size)
        return jnp.pad(
            split.transpose(0, 1, 3, 2, 4), ((0, 0),) * 4 + ((0, depth - width // size),)
        ).reshape(rows, size * depth)

    far_first, rest = swap(upper, 8), lower
    across, along = swap(state, 2), swap(state, 4)
    near_blocks = list(by_group(upper, lower))
    near_blocks[1], near_blocks[3] = swap(near_blocks[1], 2), swap(near_blocks[3], 6)
    gate_up = turned(gate_up_weight[0, 0].T)
    tokens = [columns_of(state)]
    ids, logits = expert_ids[0], gate_logits[0]
    choice = jnp.concatenate([ids.astype(F32), logits], axis=1)
    pairs = half * 4 + (own ^ jnp.arange(4, dtype=jnp.int32))
    at_pair = pairs[:, None] == jnp.arange(experts_count, dtype=jnp.int32)[None, :]
    reach = jnp.sum(jnp.where(at_pair, placement, 0), axis=1)
    hot, gates_own = routing(ids, logits, reach, slots)
    near_blocks, far_first, rest, across, along, gate_up, down, tokens, hot, gates_own, choice = (
        lax.optimization_barrier(
            (near_blocks, far_first, rest, across, along)
            + (gate_up, down, tokens, hot, gates_own, choice)
        )
    )
    weight_far = (far_first, swap(rest, 8))
    corner = swap(along, 2)
    near_blocks[2] = swap(near_blocks[2], 4)
    gate_up_other, down_other = swap(gate_up, 1), swap(down, 1)
    tokens += [columns_of(across), columns_of(along)]
    near_blocks, weight_far, corner, tokens, choice = lax.optimization_barrier(
        (near_blocks, weight_far, corner, tokens, choice)
    )
    near_mine = jnp.stack(near_blocks)
    near_theirs = swap(near_mine, 1)
    far_blocks = spread_out(by_group(*weight_far))
    far_choice = swap(choice, 8)
    tokens += [columns_of(corner)]

    total_shape = jax.ShapeDtypeStruct((4 * rows, GROUP_COLS), F32)
    total = pl.pallas_call(
        project_near,
        out_shape=total_shape,
        in_specs=[SMEM_SPEC] + [VMEM_SPEC] * 6,
        out_specs=VMEM_SPEC,
        compiler_params=params(),
        name="project_near",
    )(where, *tokens, near_mine, near_theirs)
    total, far_blocks, far_choice = lax.optimization_barrier((total, far_blocks, far_choice))
    far_mine = jnp.stack(far_blocks)
    far_theirs = swap(far_mine, 1)
    total = pl.pallas_call(
        project_more,
        out_shape=total_shape,
        in_specs=[SMEM_SPEC] + [VMEM_SPEC] * 6,
        out_specs=VMEM_SPEC,
        compiler_params=params(),
        name="project_more",
    )(where, *tokens, far_mine, total)
    queries, keyvals = pl.pallas_call(
        project_last,
        out_shape=(
            jax.ShapeDtypeStruct((4, rows, QUERY_COLS), BF16),
            jax.ShapeDtypeStruct((4, rows, 2 * HEAD_DIM), BF16),
        ),
        in_specs=[SMEM_SPEC] + [VMEM_SPEC] * 7,
        out_specs=(VMEM_SPEC, VMEM_SPEC),
        compiler_params=params(),
        name="project_last",
    )(where, *tokens, far_theirs, total, bias)

    partner = swap(keyvals, 1)
    rim = lax.ppermute(
        keyvals[3], "expert", [(i, i + 7) for i in range(size - 8) if i & 1]
    )
    behind = jnp.concatenate([rim[None], partner], axis=0)
    attended = pl.pallas_call(
        attend,
        out_shape=jax.ShapeDtypeStruct((4, rows, QUERY_COLS), BF16),
        in_specs=[SMEM_SPEC] + [VMEM_SPEC] * 3 + [SMEM_SPEC],
        out_specs=VMEM_SPEC,
        compiler_params=params(),
        name="attend",
    )(where, queries, keyvals, behind, attention_sink_logits[0])
    heads = spread_out([pick(attended, r) for r in range(4)])
    far_hot, gates_far = routing(
        far_choice[:, :TOP].astype(jnp.int32), far_choice[:, TOP:], reach, slots
    )
    heads, far_hot, gates_far = lax.optimization_barrier((heads, far_hot, gates_far))
    by_head = jnp.zeros((rows, QUERY_HEADS * HEAD_DIM), BF16)
    for r in range(4):
        by_head = lax.dynamic_update_slice(by_head, heads[r], (0, (own ^ r) * QUERY_COLS))
    residual = (
        state.astype(F32)
        + jnp.dot(by_head, out_weight[0], preferred_element_type=F32)
        + out_bias[0]
    ).astype(BF16)
    normed_mid = normed(residual, expert_gain[0])
    normed_mid, gate_up_other, down_other = lax.optimization_barrier(
        (normed_mid, gate_up_other, down_other)
    )

    tiles = [(gate_up, down), (gate_up_other, down_other)]
    far_mid = swap(normed_mid, 8)
    near_rows = spread_out(list(packed(hot, normed_mid)))
    far_rows = spread_out(list(packed(far_hot, far_mid)))
    cut = (width // 256 + 1) * 128
    spans = ((0, cut), (cut, width))
    (early,) = expert(near_rows + far_rows[:1], tiles, ((0, width),), "near_expert")
    far_rows, early = lax.optimization_barrier((far_rows, early))
    near_out, far_own = early[:4], early[4]
    near_back = spread_out(near_out)
    first, second = expert(far_rows[1:], tiles, spans, "far_expert")
    near_back, first, second = lax.optimization_barrier((near_back, first, second))
    first = [far_own[:, :cut]] + [swap(first[r - 1], 2 * r) for r in range(1, 4)]
    first, second = lax.optimization_barrier((first, second))
    second = [far_own[:, cut:]] + [swap(second[r - 1], 2 * r) for r in range(1, 4)]
    far_sum = [
        unpacked(far_hot, gates_far, jnp.stack(back)).astype(BF16) for back in (first, second)
    ]

    sections = lax.axis_size("section")
    ahead = [
        (s * size + i, (s + 1) % sections * size + (i ^ 8))
        for s in range(sections)
        for i in range(size)
    ]
    far_sum = jnp.concatenate(
        [lax.ppermute(part, ("section", "expert"), ahead) for part in far_sum], axis=1
    )
    near_sum = unpacked(hot, gates_own, jnp.stack(near_back))
    near_sum = (residual.astype(F32) + near_sum).astype(BF16)
    near_sum = lax.ppermute(
        near_sum, "section", [(s, (s + 1) % sections) for s in range(sections)]
    )
    return (near_sum.astype(F32) + far_sum.astype(F32)).astype(BF16)[None]


def solution(mesh):
    return jax.shard_map(
        shards,
        mesh=mesh,
        in_specs=(
            P("section", "expert", None),
            P("section", None),
            P("section", "expert", None),
            P("section", None),
            P("section", None, None),
            P("section", None),
            P("section", None),
            P("section", None),
            P("section", "expert", None, None),
            P("section", "expert", None, None),
            P("section", "expert", None),
            P("section", "expert", None),
            P("section", None),
        ),
        out_specs=P("section", "expert", None),
        check_vma=False,
    )
```

```python
import functools

import jax
import jax.numpy as jnp
from jax import lax
from jax.experimental import pallas as pl
from jax.experimental.pallas import tpu as pltpu
from jax.sharding import PartitionSpec as P

HEAD_DIM = 64
QUERY_HEADS = 32
KEY_VALUE_HEADS = 4
WINDOW_TOKENS = 128
TOP = 4
GROUP = QUERY_HEADS // KEY_VALUE_HEADS
QUERY_COLS = GROUP * HEAD_DIM
GROUP_COLS = QUERY_COLS + 2 * HEAD_DIM
BF16 = jnp.bfloat16
F32 = jnp.float32
VMEM_BYTES = 50 * 1024 * 1024


def swap(x, mask):
    size = lax.axis_size("expert")
    return lax.ppermute(x, "expert", [(i, i ^ mask) for i in range(size)])


def normed(vector, gain_row):
    as_float = vector.astype(F32)
    inverse_rms = lax.rsqrt(jnp.mean(as_float * as_float, axis=-1, keepdims=True) + 1e-05)
    return (as_float * inverse_rms * gain_row).astype(BF16)


def params(limit=VMEM_BYTES):
    return pltpu.CompilerParams(vmem_limit_bytes=limit)


SMEM_SPEC = pl.BlockSpec(memory_space=pltpu.SMEM)
VMEM_SPEC = pl.BlockSpec(memory_space=pltpu.VMEM)


def regroup(where, upper, lower, *blocks):
    own = where[1]
    query_end = QUERY_HEADS * HEAD_DIM
    middle = upper.shape[0]
    for part, lines in ((upper, pl.ds(0, middle)), (lower, pl.ds(middle, lower.shape[0]))):
        for r in range(4):
            group = own ^ r
            odd = (group & 1) == 1
            queries = part[:, pl.ds(pl.multiple_of(group * QUERY_COLS, 128), QUERY_COLS)]
            halves = []
            for start in (query_end, query_end + KEY_VALUE_HEADS * HEAD_DIM):
                at = pl.multiple_of(start + (group >> 1) * 2 * HEAD_DIM, 128)
                pair = part[:, pl.ds(at, 2 * HEAD_DIM)]
                halves.append(jnp.where(odd, pair[:, HEAD_DIM:], pair[:, :HEAD_DIM]))
            blocks[r][lines, :QUERY_COLS] = queries
            blocks[r][lines, QUERY_COLS:] = jnp.concatenate(halves, axis=1)


def project_rows(base, own, tokens, weights):
    depth = weights.shape[1]
    odd = (own & 1) == 1
    total = None
    for r in (0, 2):
        pair = (weights[r], weights[r + 1])
        ordered = jnp.concatenate(
            [jnp.where(odd, pair[1], pair[0]), jnp.where(odd, pair[0], pair[1])], axis=0
        )
        start = pl.multiple_of((base * 4 + ((own & 2) ^ r)) * depth, 128)
        columns = pl.ds(start, 2 * depth)
        stacked = jnp.concatenate([t[:, columns] for t in tokens], axis=0)
        part = jnp.dot(stacked, ordered, preferred_element_type=F32)
        total = part if total is None else total + part
    return total


def project_near(where, t0, t1, t2, t3, mine, theirs, out):
    half, own, core = where[0], where[1], where[2]
    tokens = (t0, t1, t2, t3)
    out[...] = project_rows(2 * half + core, own, tokens, mine) + project_rows(
        2 * half + 1 - core, own, tokens, theirs
    )


def project_more(where, t0, t1, t2, t3, mine, before, out):
    half, own, core = where[0], where[1], where[2]
    tokens = (t0, t1, t2, t3)
    out[...] = before[...] + project_rows(2 * (1 - half) + core, own, tokens, mine)


def project_last(where, t0, t1, t2, t3, theirs, before, bias, queries, keyvals):
    half, own, core = where[0], where[1], where[2]
    tokens = (t0, t1, t2, t3)
    total = before[...] + project_rows(2 * (1 - half) + 1 - core, own, tokens, theirs)
    rows = t0.shape[0]
    projected = (total + bias[pl.ds(own, 1), :]).astype(BF16)
    for r in range(4):
        block = projected[r * rows : (r + 1) * rows]
        queries[own ^ r] = block[:, :QUERY_COLS]
        keyvals[own ^ r] = block[:, QUERY_COLS:]


def attend(blocks, where, queries, keyvals, partner, rim, sinks, *refs):
    out = refs[-1]
    if len(refs) == 2:
        out[...] = refs[0][...]
    half, own, core = where[0], where[1], where[2]
    rows = queries.shape[1]
    shape = (2 * rows, GROUP * rows)
    key_at = lax.broadcasted_iota(jnp.int32, shape, 0)
    distance = lax.rem(lax.broadcasted_iota(jnp.int32, shape, 1), rows) - key_at + rows
    band = (distance >= 0) & (distance < WINDOW_TOKENS)
    sink = jnp.concatenate(
        [jnp.full((1, rows), sinks[own * GROUP + j], F32) for j in range(GROUP)], axis=1
    )
    for b in blocks:
        before = partner[b - 1 + core] if b else jnp.where(core == 0, rim[...], partner[0])
        both = jnp.concatenate([before, keyvals[b]], axis=0)
        turned = queries[b].T
        heads = jnp.concatenate(
            [turned[j * HEAD_DIM : (j + 1) * HEAD_DIM] for j in range(GROUP)], axis=1
        )
        scores = jnp.dot(both[:, :HEAD_DIM], heads, preferred_element_type=F32) * 0.125
        inside = band
        if b == 0:
            first_key = jnp.where((half == 0) & (core == 0), rows, 0)
            inside = band & (key_at >= first_key)
        masked = jnp.where(inside, scores, -1e30)
        peak = jnp.maximum(jnp.max(masked, axis=0, keepdims=True), sink)
        numer = jnp.where(inside, jnp.exp(masked - peak), 0.0)
        denominator = jnp.sum(numer, axis=0, keepdims=True) + jnp.exp(sink - peak)
        weights = (numer / denominator).astype(BF16)
        mixed = lax.dot_general(
            both[:, HEAD_DIM:], weights, (((0,), (0,)), ((), ())), preferred_element_type=F32
        ).astype(BF16)
        out[b] = jnp.concatenate(
            [mixed[:, j * rows : (j + 1) * rows] for j in range(GROUP)], axis=0
        ).T


def routing(ids, logits, experts, slots):
    gates = jax.nn.softmax(logits, axis=-1)
    hits = ids[None, :, :] == experts[:, None, None]
    chosen = jnp.any(hits, axis=-1)
    weight = jnp.sum(jnp.where(hits, gates[None], 0.0), axis=-1)
    rows = ids.shape[0]
    earlier = jnp.arange(rows)[:, None] < jnp.arange(rows)[None, :]
    rank = jnp.dot(chosen.astype(BF16), earlier.astype(BF16), preferred_element_type=F32)
    slot = jnp.arange(slots, dtype=jnp.int32)
    one_hot = (rank.astype(jnp.int32)[:, None, :] == slot[None, :, None]) & chosen[:, None, :]
    return one_hot.astype(BF16), weight


def packed(one_hot, rows):
    return jnp.einsum("rst,td->rsd", one_hot, rows, preferred_element_type=F32).astype(BF16)


def unpacked(one_hot, weight, results):
    spread = jnp.einsum("rst,rsd->rtd", one_hot, results, preferred_element_type=F32)
    return jnp.sum(spread * weight[:, :, None], axis=0)


def turn_kernel(source, out):
    hid, room = source.shape[0] // 2, out.shape[1] // 2
    empty = jnp.zeros((out.shape[0], room - hid), out.dtype)
    out[:, :room] = jnp.concatenate([source[:hid].T, empty], axis=1)
    out[:, room:] = jnp.concatenate([source[hid:].T, empty], axis=1)


def turned(array):
    lines, width = array.shape
    room = 2 * -(-lines // 256) * 128
    step = 640
    return pl.pallas_call(
        turn_kernel,
        out_shape=jax.ShapeDtypeStruct((width, room), array.dtype),
        grid=(-(-width // step),),
        in_specs=[pl.BlockSpec((lines, step), lambda i: (0, i))],
        out_specs=pl.BlockSpec((step, room), lambda i: (i, 0)),
        compiler_params=params(),
        name="turned",
    )(array)


DEPTH_CHUNK = 1536


def expert_kernel(count, spans, *refs):
    blocks, sources = refs[:count], refs[count : count + 4]
    outs, (gate_up, down, total, sems) = refs[count + 4 : -4], refs[-4:]
    width, both = gate_up.shape[1:]
    room, hid = both // 2, down.shape[1]
    starts = list(range(0, width, DEPTH_CHUNK))
    up_copies, down_copies = [], []
    for tile in range(2):
        up_copies.append(
            [
                pltpu.make_async_copy(
                    sources[2 * tile].at[pl.ds(at, min(DEPTH_CHUNK, width - at))],
                    gate_up.at[tile, pl.ds(at, min(DEPTH_CHUNK, width - at))],
                    sems.at[tile, n],
                )
                for n, at in enumerate(starts)
            ]
        )
        down_copies.append(
            pltpu.make_async_copy(
                sources[2 * tile + 1], down.at[tile], sems.at[tile, len(starts)]
            )
        )
    for tile in range(2):
        for copy in up_copies[tile]:
            copy.start()
        down_copies[tile].start()
    rows = jnp.concatenate([block[...] for block in blocks], axis=0)
    for tile in range(2):
        hidden = None
        for copy, at in zip(up_copies[tile], starts):
            copy.wait()
            end = min(at + DEPTH_CHUNK, width)
            part = jnp.dot(rows[:, at:end], gate_up[tile, at:end], preferred_element_type=F32)
            hidden = part if hidden is None else hidden + part
        gate, up = hidden[:, :room], hidden[:, room:]
        act = ((up + 1.0) * gate * jax.nn.sigmoid(1.702 * gate)).astype(BF16)
        down_copies[tile].wait()
        part = jnp.dot(act[:, :hid], down[tile], preferred_element_type=F32).astype(BF16)
        if tile == 0:
            total[...] = part
    summed = (total[...].astype(F32) + part.astype(F32)).astype(BF16)
    slots = blocks[0].shape[0]
    for n, out in enumerate(outs):
        block, (start, end) = n % count, spans[n // count]
        out[...] = summed[block * slots : (block + 1) * slots, start:end]


def expert(blocks, tiles, spans, name):
    count = len(blocks)
    slots, width = blocks[0].shape
    hid = tiles[0][1].shape[0]
    any_spec = pl.BlockSpec(memory_space=pl.ANY)
    outs = pl.pallas_call(
        functools.partial(expert_kernel, count, spans),
        out_shape=[
            jax.ShapeDtypeStruct((slots, end - start), BF16)
            for start, end in spans
            for _ in blocks
        ],
        in_specs=[VMEM_SPEC] * count + [any_spec] * 4,
        out_specs=[VMEM_SPEC] * (count * len(spans)),
        scratch_shapes=[
            pltpu.VMEM((2, width, tiles[0][0].shape[1]), BF16),
            pltpu.VMEM((2, hid, width), BF16),
            pltpu.VMEM((count * slots, width), BF16),
            pltpu.SemaphoreType.DMA((2, -(-width // DEPTH_CHUNK) + 1)),
        ],
        compiler_params=params(),
        cost_estimate=pl.CostEstimate(
            flops=2 * 2 * count * slots * width * 3 * hid,
            bytes_accessed=2 * 2 * 3 * hid * width + 4 * count * slots * width,
            transcendentals=2 * count * slots * hid,
        ),
        name=name,
    )(*blocks, *tiles[0], *tiles[1])
    return [list(outs[n * count : (n + 1) * count]) for n in range(len(spans))]


def spread_out(blocks):
    return [blocks[0]] + [swap(blocks[r], 2 * r) for r in range(1, 4)]


def shards(
    section_input,
    attention_gain,
    query_key_value_weight,
    qkv_bias,
    out_weight,
    out_bias,
    attention_sink_logits,
    expert_gain,
    gate_up_weight,
    down_weight,
    expert_ids,
    gate_logits,
    placement,
):
    rows, width = section_input.shape[1:]
    experts_count = placement.shape[1]
    slots = 2 * min(rows // 2, rows * TOP * 5 // (8 * experts_count))
    me = lax.axis_index("expert").astype(jnp.int32)
    half, own, core = me >> 3, (me >> 1) & 3, me & 1
    where = jnp.stack([half, own, core])
    state = section_input[0]

    weight = query_key_value_weight[0]
    weight_rows = weight.shape[0]
    depth = -(-weight_rows // 64) * 64
    query_end = QUERY_HEADS * HEAD_DIM
    key_end = query_end + KEY_VALUE_HEADS * HEAD_DIM

    def grouped(array):
        lead = array.shape[0]
        return jnp.concatenate(
            [
                array[:, :query_end].reshape(lead, 4, QUERY_COLS),
                array[:, query_end:key_end].reshape(lead, 4, HEAD_DIM),
                array[:, key_end:].reshape(lead, 4, HEAD_DIM),
            ],
            axis=2,
        )

    bias = grouped(qkv_bias)[0]
    pick = lambda array, r: lax.dynamic_index_in_dim(array, own ^ r, 0, keepdims=False)
    down = down_weight[0, 0]

    size = lax.axis_size("expert")
    first_rows = depth // 32 * 16 + 16
    upper = weight[:first_rows]
    lower = jnp.pad(weight[first_rows:], ((0, depth - weight_rows), (0, 0)))

    def by_group(upper, lower):
        return pl.pallas_call(
            regroup,
            out_shape=(jax.ShapeDtypeStruct((depth, GROUP_COLS), BF16),) * 4,
            in_specs=[SMEM_SPEC, VMEM_SPEC, VMEM_SPEC],
            out_specs=(VMEM_SPEC,) * 4,
            compiler_params=params(),
            name="regroup",
        )(where, upper, lower)

    def columns_of(tokens):
        split = normed(tokens, attention_gain[0]).reshape(rows, 2, 4, 2, width // size)
        return jnp.pad(
            split.transpose(0, 1, 3, 2, 4), ((0, 0),) * 4 + ((0, depth - width // size),)
        ).reshape(rows, size * depth)

    far_first, rest = swap(upper, 8), lower
    across, along = swap(state, 2), swap(state, 4)
    near_blocks = list(by_group(upper, lower))
    near_blocks[1], near_blocks[3] = swap(near_blocks[1], 2), swap(near_blocks[3], 6)
    gate_up = turned(gate_up_weight[0, 0].T)
    tokens = [columns_of(state)]
    ids, logits = expert_ids[0], gate_logits[0]
    choice = jnp.concatenate([ids.astype(F32), logits], axis=1)
    pairs = half * 4 + (own ^ jnp.arange(4, dtype=jnp.int32))
    at_pair = pairs[:, None] == jnp.arange(experts_count, dtype=jnp.int32)[None, :]
    reach = jnp.sum(jnp.where(at_pair, placement, 0), axis=1)
    hot, gates_own = routing(ids, logits, reach, slots)
    near_blocks, far_first, rest, across, along, gate_up, down, tokens, hot, gates_own, choice = (
        lax.optimization_barrier(
            (near_blocks, far_first, rest, across, along)
            + (gate_up, down, tokens, hot, gates_own, choice)
        )
    )
    weight_far = (far_first, swap(rest, 8))
    corner = swap(along, 2)
    near_blocks[2] = swap(near_blocks[2], 4)
    gate_up_other, down_other = swap(gate_up, 1), swap(down, 1)
    tokens += [columns_of(across), columns_of(along)]
    near_blocks, weight_far, corner, tokens, choice = lax.optimization_barrier(
        (near_blocks, weight_far, corner, tokens, choice)
    )
    near_mine = jnp.stack(near_blocks)
    near_theirs = swap(near_mine, 1)
    far_blocks = spread_out(by_group(*weight_far))
    far_choice = swap(choice, 8)
    tokens += [columns_of(corner)]

    total_shape = jax.ShapeDtypeStruct((4 * rows, GROUP_COLS), F32)
    total = pl.pallas_call(
        project_near,
        out_shape=total_shape,
        in_specs=[SMEM_SPEC] + [VMEM_SPEC] * 6,
        out_specs=VMEM_SPEC,
        compiler_params=params(),
        name="project_near",
    )(where, *tokens, near_mine, near_theirs)
    total, far_blocks, far_choice = lax.optimization_barrier((total, far_blocks, far_choice))
    far_mine = jnp.stack(far_blocks)
    far_theirs = swap(far_mine, 1)
    total = pl.pallas_call(
        project_more,
        out_shape=total_shape,
        in_specs=[SMEM_SPEC] + [VMEM_SPEC] * 6,
        out_specs=VMEM_SPEC,
        compiler_params=params(),
        name="project_more",
    )(where, *tokens, far_mine, total)
    queries, keyvals = pl.pallas_call(
        project_last,
        out_shape=(
            jax.ShapeDtypeStruct((4, rows, QUERY_COLS), BF16),
            jax.ShapeDtypeStruct((4, rows, 2 * HEAD_DIM), BF16),
        ),
        in_specs=[SMEM_SPEC] + [VMEM_SPEC] * 7,
        out_specs=(VMEM_SPEC, VMEM_SPEC),
        compiler_params=params(),
        name="project_last",
    )(where, *tokens, far_theirs, total, bias)

    partner = swap(keyvals, 1)
    rim = swap(keyvals[3], 9)

    def attend_blocks(blocks, rim, *done):
        return pl.pallas_call(
            functools.partial(attend, blocks),
            out_shape=jax.ShapeDtypeStruct((4, rows, QUERY_COLS), BF16),
            in_specs=[SMEM_SPEC] + [VMEM_SPEC] * 4 + [SMEM_SPEC] + [VMEM_SPEC] * len(done),
            out_specs=VMEM_SPEC,
            compiler_params=params(),
            name="attend",
        )(where, queries, keyvals, partner, rim, attention_sink_logits[0], *done)

    attended = attend_blocks((0,), rim, attend_blocks((1, 2, 3), partner[0]))
    heads = spread_out([pick(attended, r) for r in range(4)])
    far_hot, gates_far = routing(
        far_choice[:, :TOP].astype(jnp.int32), far_choice[:, TOP:], reach, slots
    )
    heads, far_hot, gates_far = lax.optimization_barrier((heads, far_hot, gates_far))
    by_head = jnp.zeros((rows, QUERY_HEADS * HEAD_DIM), BF16)
    for r in range(4):
        by_head = lax.dynamic_update_slice(by_head, heads[r], (0, (own ^ r) * QUERY_COLS))
    residual = (
        state.astype(F32)
        + jnp.dot(by_head, out_weight[0], preferred_element_type=F32)
        + out_bias[0]
    ).astype(BF16)
    normed_mid = normed(residual, expert_gain[0])
    normed_mid, gate_up_other, down_other = lax.optimization_barrier(
        (normed_mid, gate_up_other, down_other)
    )

    tiles = [(gate_up, down), (gate_up_other, down_other)]
    far_mid = swap(normed_mid, 8)
    near_rows = spread_out(list(packed(hot, normed_mid)))
    far_rows = spread_out(list(packed(far_hot, far_mid)))
    cut = (width // 256 + 1) * 128
    spans = ((0, cut), (cut, width))
    (near_out,) = expert(near_rows, tiles, ((0, width),), "near_expert")
    far_rows, _ = lax.optimization_barrier((far_rows, near_out))
    near_back = spread_out(near_out)
    first, second = expert(far_rows, tiles, spans, "far_expert")
    near_back, first, second = lax.optimization_barrier((near_back, first, second))
    first = spread_out(first)
    first, second = lax.optimization_barrier((first, second))
    second = spread_out(second)
    far_sum = [
        unpacked(far_hot, gates_far, jnp.stack(back)).astype(BF16) for back in (first, second)
    ]

    sections = lax.axis_size("section")
    ahead = [
        (s * size + i, (s + 1) % sections * size + (i ^ 8))
        for s in range(sections)
        for i in range(size)
    ]
    far_sum = jnp.concatenate(
        [lax.ppermute(part, ("section", "expert"), ahead) for part in far_sum], axis=1
    )
    near_sum = unpacked(hot, gates_own, jnp.stack(near_back))
    near_sum = (residual.astype(F32) + near_sum).astype(BF16)
    near_sum = lax.ppermute(
        near_sum, "section", [(s, (s + 1) % sections) for s in range(sections)]
    )
    return (near_sum.astype(F32) + far_sum.astype(F32)).astype(BF16)[None]


def solution(mesh):
    return jax.shard_map(
        shards,
        mesh=mesh,
        in_specs=(
            P("section", "expert", None),
            P("section", None),
            P("section", "expert", None),
            P("section", None),
            P("section", None, None),
            P("section", None),
            P("section", None),
            P("section", None),
            P("section", "expert", None, None),
            P("section", "expert", None, None),
            P("section", "expert", None),
            P("section", "expert", None),
            P("section", None),
        ),
        out_specs=P("section", "expert", None),
        check_vma=False,
    )
```

```python
import functools

import jax
import jax.numpy as jnp
from jax import lax
from jax.experimental import pallas as pl
from jax.experimental.pallas import tpu as pltpu
from jax.sharding import PartitionSpec as P

HEAD_DIM = 64
QUERY_HEADS = 32
KEY_VALUE_HEADS = 4
WINDOW_TOKENS = 128
TOP = 4
GROUP = QUERY_HEADS // KEY_VALUE_HEADS
QUERY_COLS = GROUP * HEAD_DIM
GROUP_COLS = QUERY_COLS + 2 * HEAD_DIM
BF16 = jnp.bfloat16
F32 = jnp.float32
VMEM_BYTES = 20 * 1024 * 1024
EXPERT_VMEM_BYTES = 48 * 1024 * 1024


def swap(x, mask):
    size = lax.axis_size("expert")
    return lax.ppermute(x, "expert", [(i, i ^ mask) for i in range(size)])


def normed(vector, gain_row):
    as_float = vector.astype(F32)
    inverse_rms = lax.rsqrt(jnp.mean(as_float * as_float, axis=-1, keepdims=True) + 1e-05)
    return (as_float * inverse_rms * gain_row).astype(BF16)


def params(limit=VMEM_BYTES):
    return pltpu.CompilerParams(vmem_limit_bytes=limit)


SMEM_SPEC = pl.BlockSpec(memory_space=pltpu.SMEM)
VMEM_SPEC = pl.BlockSpec(memory_space=pltpu.VMEM)


def regroup(where, upper, lower, *blocks):
    own = where[1]
    query_end = QUERY_HEADS * HEAD_DIM
    middle = upper.shape[0]
    for part, lines in ((upper, pl.ds(0, middle)), (lower, pl.ds(middle, lower.shape[0]))):
        for r in range(4):
            group = own ^ r
            odd = (group & 1) == 1
            queries = part[:, pl.ds(pl.multiple_of(group * QUERY_COLS, 128), QUERY_COLS)]
            halves = []
            for start in (query_end, query_end + KEY_VALUE_HEADS * HEAD_DIM):
                at = pl.multiple_of(start + (group >> 1) * 2 * HEAD_DIM, 128)
                pair = part[:, pl.ds(at, 2 * HEAD_DIM)]
                halves.append(jnp.where(odd, pair[:, HEAD_DIM:], pair[:, :HEAD_DIM]))
            blocks[r][lines, :QUERY_COLS] = queries
            blocks[r][lines, QUERY_COLS:] = jnp.concatenate(halves, axis=1)


def project_rows(base, own, tokens, weights):
    depth = weights.shape[1]
    odd = (own & 1) == 1
    total = None
    for r in (0, 2):
        pair = (weights[r], weights[r + 1])
        ordered = jnp.concatenate(
            [jnp.where(odd, pair[1], pair[0]), jnp.where(odd, pair[0], pair[1])], axis=0
        )
        start = pl.multiple_of((base * 4 + ((own & 2) ^ r)) * depth, 128)
        columns = pl.ds(start, 2 * depth)
        stacked = jnp.concatenate([t[:, columns] for t in tokens], axis=0)
        part = jnp.dot(stacked, ordered, preferred_element_type=F32)
        total = part if total is None else total + part
    return total


def project_near(where, t0, t1, t2, t3, mine, theirs, out):
    half, own, core = where[0], where[1], where[2]
    tokens = (t0, t1, t2, t3)
    out[...] = project_rows(2 * half + core, own, tokens, mine) + project_rows(
        2 * half + 1 - core, own, tokens, theirs
    )


def project_more(where, t0, t1, t2, t3, mine, before, out):
    half, own, core = where[0], where[1], where[2]
    tokens = (t0, t1, t2, t3)
    out[...] = before[...] + project_rows(2 * (1 - half) + core, own, tokens, mine)


def project_last(where, t0, t1, t2, t3, theirs, before, bias, queries, keyvals):
    half, own, core = where[0], where[1], where[2]
    tokens = (t0, t1, t2, t3)
    total = before[...] + project_rows(2 * (1 - half) + 1 - core, own, tokens, theirs)
    rows = t0.shape[0]
    projected = (total + bias[pl.ds(own, 1), :]).astype(BF16)
    for r in range(4):
        block = projected[r * rows : (r + 1) * rows]
        queries[own ^ r] = block[:, :QUERY_COLS]
        keyvals[own ^ r] = block[:, QUERY_COLS:]


def attend(blocks, where, queries, keyvals, partner, rim, sinks, *refs):
    out = refs[-1]
    if len(refs) == 2:
        out[...] = refs[0][...]
    half, own, core = where[0], where[1], where[2]
    rows = queries.shape[1]
    shape = (2 * rows, GROUP * rows)
    key_at = lax.broadcasted_iota(jnp.int32, shape, 0)
    distance = lax.rem(lax.broadcasted_iota(jnp.int32, shape, 1), rows) - key_at + rows
    band = (distance >= 0) & (distance < WINDOW_TOKENS)
    sink = jnp.concatenate(
        [jnp.full((1, rows), sinks[own * GROUP + j], F32) for j in range(GROUP)], axis=1
    )
    for b in blocks:
        before = partner[b - 1 + core] if b else jnp.where(core == 0, rim[...], partner[0])
        both = jnp.concatenate([before, keyvals[b]], axis=0)
        turned = queries[b].T
        heads = jnp.concatenate(
            [turned[j * HEAD_DIM : (j + 1) * HEAD_DIM] for j in range(GROUP)], axis=1
        )
        scores = jnp.dot(both[:, :HEAD_DIM], heads, preferred_element_type=F32) * 0.125
        inside = band
        if b == 0:
            first_key = jnp.where((half == 0) & (core == 0), rows, 0)
            inside = band & (key_at >= first_key)
        masked = jnp.where(inside, scores, -1e30)
        peak = jnp.maximum(jnp.max(masked, axis=0, keepdims=True), sink)
        numer = jnp.where(inside, jnp.exp(masked - peak), 0.0)
        denominator = jnp.sum(numer, axis=0, keepdims=True) + jnp.exp(sink - peak)
        weights = (numer / denominator).astype(BF16)
        mixed = lax.dot_general(
            both[:, HEAD_DIM:], weights, (((0,), (0,)), ((), ())), preferred_element_type=F32
        ).astype(BF16)
        out[b] = jnp.concatenate(
            [mixed[:, j * rows : (j + 1) * rows] for j in range(GROUP)], axis=0
        ).T


def routing(ids, logits, experts, slots):
    gates = jax.nn.softmax(logits, axis=-1)
    hits = ids[None, :, :] == experts[:, None, None]
    chosen = jnp.any(hits, axis=-1)
    weight = jnp.sum(jnp.where(hits, gates[None], 0.0), axis=-1)
    rows = ids.shape[0]
    earlier = jnp.arange(rows)[:, None] < jnp.arange(rows)[None, :]
    rank = jnp.dot(chosen.astype(BF16), earlier.astype(BF16), preferred_element_type=F32)
    slot = jnp.arange(slots, dtype=jnp.int32)
    one_hot = (rank.astype(jnp.int32)[:, None, :] == slot[None, :, None]) & chosen[:, None, :]
    return one_hot.astype(BF16), weight


def packed(one_hot, rows):
    return jnp.einsum("rst,td->rsd", one_hot, rows, preferred_element_type=F32).astype(BF16)


def unpacked(one_hot, weight, results):
    spread = jnp.einsum("rst,rsd->rtd", one_hot, results, preferred_element_type=F32)
    return jnp.sum(spread * weight[:, :, None], axis=0)


def turn_kernel(source, out):
    hid, room = source.shape[0] // 2, out.shape[1] // 2
    empty = jnp.zeros((out.shape[0], room - hid), out.dtype)
    out[:, :room] = jnp.concatenate([source[:hid].T, empty], axis=1)
    out[:, room:] = jnp.concatenate([source[hid:].T, empty], axis=1)


def turned(array):
    lines, width = array.shape
    room = 2 * -(-lines // 256) * 128
    step = 640
    return pl.pallas_call(
        turn_kernel,
        out_shape=jax.ShapeDtypeStruct((width, room), array.dtype),
        grid=(-(-width // step),),
        in_specs=[pl.BlockSpec((lines, step), lambda i: (0, i))],
        out_specs=pl.BlockSpec((step, room), lambda i: (i, 0)),
        compiler_params=params(),
        name="turned",
    )(array)


DEPTH_CHUNK = 1536


def expert_kernel(count, spans, *refs):
    blocks, sources = refs[:count], refs[count : count + 4]
    outs, (gate_up, down, total, sems) = refs[count + 4 : -4], refs[-4:]
    width, both = gate_up.shape[1:]
    room, hid = both // 2, down.shape[1]
    starts = list(range(0, width, DEPTH_CHUNK))
    up_copies, down_copies = [], []
    for tile in range(2):
        up_copies.append(
            [
                pltpu.make_async_copy(
                    sources[2 * tile].at[pl.ds(at, min(DEPTH_CHUNK, width - at))],
                    gate_up.at[tile, pl.ds(at, min(DEPTH_CHUNK, width - at))],
                    sems.at[tile, n],
                )
                for n, at in enumerate(starts)
            ]
        )
        down_copies.append(
            pltpu.make_async_copy(
                sources[2 * tile + 1], down.at[tile], sems.at[tile, len(starts)]
            )
        )
    for tile in range(2):
        for copy in up_copies[tile]:
            copy.start()
        down_copies[tile].start()
    rows = jnp.concatenate([block[...] for block in blocks], axis=0)
    for tile in range(2):
        hidden = None
        for copy, at in zip(up_copies[tile], starts):
            copy.wait()
            end = min(at + DEPTH_CHUNK, width)
            part = jnp.dot(rows[:, at:end], gate_up[tile, at:end], preferred_element_type=F32)
            hidden = part if hidden is None else hidden + part
        gate, up = hidden[:, :room], hidden[:, room:]
        act = ((up + 1.0) * gate * jax.nn.sigmoid(1.702 * gate)).astype(BF16)
        down_copies[tile].wait()
        part = jnp.dot(act[:, :hid], down[tile], preferred_element_type=F32).astype(BF16)
        if tile == 0:
            total[...] = part
    summed = (total[...].astype(F32) + part.astype(F32)).astype(BF16)
    slots = blocks[0].shape[0]
    for n, out in enumerate(outs):
        block, (start, end) = n % count, spans[n // count]
        out[...] = summed[block * slots : (block + 1) * slots, start:end]


def expert(blocks, tiles, spans, name):
    count = len(blocks)
    slots, width = blocks[0].shape
    hid = tiles[0][1].shape[0]
    any_spec = pl.BlockSpec(memory_space=pl.ANY)
    outs = pl.pallas_call(
        functools.partial(expert_kernel, count, spans),
        out_shape=[
            jax.ShapeDtypeStruct((slots, end - start), BF16)
            for start, end in spans
            for _ in blocks
        ],
        in_specs=[VMEM_SPEC] * count + [any_spec] * 4,
        out_specs=[VMEM_SPEC] * (count * len(spans)),
        scratch_shapes=[
            pltpu.VMEM((2, width, tiles[0][0].shape[1]), BF16),
            pltpu.VMEM((2, hid, width), BF16),
            pltpu.VMEM((count * slots, width), BF16),
            pltpu.SemaphoreType.DMA((2, -(-width // DEPTH_CHUNK) + 1)),
        ],
        compiler_params=params(EXPERT_VMEM_BYTES),
        cost_estimate=pl.CostEstimate(
            flops=2 * 2 * count * slots * width * 3 * hid,
            bytes_accessed=2 * 2 * 3 * hid * width + 4 * count * slots * width,
            transcendentals=2 * count * slots * hid,
        ),
        name=name,
    )(*blocks, *tiles[0], *tiles[1])
    return [list(outs[n * count : (n + 1) * count]) for n in range(len(spans))]


def spread_out(blocks):
    return [blocks[0]] + [swap(blocks[r], 2 * r) for r in range(1, 4)]


def shards(
    section_input,
    attention_gain,
    query_key_value_weight,
    qkv_bias,
    out_weight,
    out_bias,
    attention_sink_logits,
    expert_gain,
    gate_up_weight,
    down_weight,
    expert_ids,
    gate_logits,
    placement,
):
    rows, width = section_input.shape[1:]
    experts_count = placement.shape[1]
    slots = 2 * min(rows // 2, rows * TOP * 5 // (8 * experts_count))
    me = lax.axis_index("expert").astype(jnp.int32)
    half, own, core = me >> 3, (me >> 1) & 3, me & 1
    where = jnp.stack([half, own, core])
    state = section_input[0]

    weight = query_key_value_weight[0]
    weight_rows = weight.shape[0]
    depth = -(-weight_rows // 64) * 64
    query_end = QUERY_HEADS * HEAD_DIM
    key_end = query_end + KEY_VALUE_HEADS * HEAD_DIM

    def grouped(array):
        lead = array.shape[0]
        return jnp.concatenate(
            [
                array[:, :query_end].reshape(lead, 4, QUERY_COLS),
                array[:, query_end:key_end].reshape(lead, 4, HEAD_DIM),
                array[:, key_end:].reshape(lead, 4, HEAD_DIM),
            ],
            axis=2,
        )

    bias = grouped(qkv_bias)[0]
    pick = lambda array, r: lax.dynamic_index_in_dim(array, own ^ r, 0, keepdims=False)
    down = down_weight[0, 0]

    size = lax.axis_size("expert")
    first_rows = depth // 32 * 16 + 16
    upper = weight[:first_rows]
    lower = jnp.pad(weight[first_rows:], ((0, depth - weight_rows), (0, 0)))

    def by_group(upper, lower):
        return pl.pallas_call(
            regroup,
            out_shape=(jax.ShapeDtypeStruct((depth, GROUP_COLS), BF16),) * 4,
            in_specs=[SMEM_SPEC, VMEM_SPEC, VMEM_SPEC],
            out_specs=(VMEM_SPEC,) * 4,
            compiler_params=params(),
            name="regroup",
        )(where, upper, lower)

    def columns_of(tokens):
        split = normed(tokens, attention_gain[0]).reshape(rows, 2, 4, 2, width // size)
        return jnp.pad(
            split.transpose(0, 1, 3, 2, 4), ((0, 0),) * 4 + ((0, depth - width // size),)
        ).reshape(rows, size * depth)

    far_first, rest = swap(upper, 8), lower
    across, along = swap(state, 2), swap(state, 4)
    near_blocks = list(by_group(upper, lower))
    near_blocks[1], near_blocks[3] = swap(near_blocks[1], 2), swap(near_blocks[3], 6)
    gate_up = turned(gate_up_weight[0, 0].T)
    tokens = [columns_of(state)]
    ids, logits = expert_ids[0], gate_logits[0]
    choice = jnp.concatenate([ids.astype(F32), logits], axis=1)
    pairs = half * 4 + (own ^ jnp.arange(4, dtype=jnp.int32))
    at_pair = pairs[:, None] == jnp.arange(experts_count, dtype=jnp.int32)[None, :]
    reach = jnp.sum(jnp.where(at_pair, placement, 0), axis=1)
    hot, gates_own = routing(ids, logits, reach, slots)
    near_blocks, far_first, rest, across, along, gate_up, down, tokens, hot, gates_own, choice = (
        lax.optimization_barrier(
            (near_blocks, far_first, rest, across, along)
            + (gate_up, down, tokens, hot, gates_own, choice)
        )
    )
    weight_far = (far_first, swap(rest, 8))
    corner = swap(along, 2)
    near_blocks[2] = swap(near_blocks[2], 4)
    gate_up_other, down_other = swap(gate_up, 1), swap(down, 1)
    tokens += [columns_of(across), columns_of(along)]
    near_blocks, weight_far, corner, tokens, choice = lax.optimization_barrier(
        (near_blocks, weight_far, corner, tokens, choice)
    )
    near_mine = jnp.stack(near_blocks)
    near_theirs = swap(near_mine, 1)
    far_blocks = spread_out(by_group(*weight_far))
    far_choice = swap(choice, 8)
    tokens += [columns_of(corner)]

    total_shape = jax.ShapeDtypeStruct((4 * rows, GROUP_COLS), F32)
    total = pl.pallas_call(
        project_near,
        out_shape=total_shape,
        in_specs=[SMEM_SPEC] + [VMEM_SPEC] * 6,
        out_specs=VMEM_SPEC,
        compiler_params=params(),
        name="project_near",
    )(where, *tokens, near_mine, near_theirs)
    total, far_blocks, far_choice = lax.optimization_barrier((total, far_blocks, far_choice))
    far_mine = jnp.stack(far_blocks)
    far_theirs = swap(far_mine, 1)
    total = pl.pallas_call(
        project_more,
        out_shape=total_shape,
        in_specs=[SMEM_SPEC] + [VMEM_SPEC] * 6,
        out_specs=VMEM_SPEC,
        compiler_params=params(),
        name="project_more",
    )(where, *tokens, far_mine, total)
    queries, keyvals = pl.pallas_call(
        project_last,
        out_shape=(
            jax.ShapeDtypeStruct((4, rows, QUERY_COLS), BF16),
            jax.ShapeDtypeStruct((4, rows, 2 * HEAD_DIM), BF16),
        ),
        in_specs=[SMEM_SPEC] + [VMEM_SPEC] * 7,
        out_specs=(VMEM_SPEC, VMEM_SPEC),
        compiler_params=params(),
        name="project_last",
    )(where, *tokens, far_theirs, total, bias)

    partner = swap(keyvals, 1)
    rim = swap(keyvals[3], 9)

    def attend_blocks(blocks, rim, *done):
        return pl.pallas_call(
            functools.partial(attend, blocks),
            out_shape=jax.ShapeDtypeStruct((4, rows, QUERY_COLS), BF16),
            in_specs=[SMEM_SPEC] + [VMEM_SPEC] * 4 + [SMEM_SPEC] + [VMEM_SPEC] * len(done),
            out_specs=VMEM_SPEC,
            compiler_params=params(),
            name="attend",
        )(where, queries, keyvals, partner, rim, attention_sink_logits[0], *done)

    attended = attend_blocks((0,), rim, attend_blocks((1, 2, 3), partner[0]))
    heads = spread_out([pick(attended, r) for r in range(4)])
    far_hot, gates_far = routing(
        far_choice[:, :TOP].astype(jnp.int32), far_choice[:, TOP:], reach, slots
    )
    heads, far_hot, gates_far = lax.optimization_barrier((heads, far_hot, gates_far))
    by_head = jnp.zeros((rows, QUERY_HEADS * HEAD_DIM), BF16)
    for r in range(4):
        by_head = lax.dynamic_update_slice(by_head, heads[r], (0, (own ^ r) * QUERY_COLS))
    residual = (
        state.astype(F32)
        + jnp.dot(by_head, out_weight[0], preferred_element_type=F32)
        + out_bias[0]
    ).astype(BF16)
    normed_mid = normed(residual, expert_gain[0])
    normed_mid, gate_up_other, down_other = lax.optimization_barrier(
        (normed_mid, gate_up_other, down_other)
    )

    tiles = [(gate_up, down), (gate_up_other, down_other)]
    far_mid = swap(normed_mid, 8)
    near_rows = spread_out(list(packed(hot, normed_mid)))
    far_rows = spread_out(list(packed(far_hot, far_mid)))
    cut = (width // 256 + 1) * 128
    spans = ((0, cut), (cut, width))
    (near_out,) = expert(near_rows, tiles, ((0, width),), "near_expert")
    far_rows, _ = lax.optimization_barrier((far_rows, near_out))
    near_back = spread_out(near_out)
    first, second = expert(far_rows, tiles, spans, "far_expert")
    near_back, first, second = lax.optimization_barrier((near_back, first, second))
    first = spread_out(first)
    first, second = lax.optimization_barrier((first, second))
    second = spread_out(second)
    far_sum = [
        unpacked(far_hot, gates_far, jnp.stack(back)).astype(BF16) for back in (first, second)
    ]

    sections = lax.axis_size("section")
    ahead = [
        (s * size + i, (s + 1) % sections * size + (i ^ 8))
        for s in range(sections)
        for i in range(size)
    ]
    far_sum = jnp.concatenate(
        [lax.ppermute(part, ("section", "expert"), ahead) for part in far_sum], axis=1
    )
    near_sum = unpacked(hot, gates_own, jnp.stack(near_back))
    near_sum = (residual.astype(F32) + near_sum).astype(BF16)
    near_sum = lax.ppermute(
        near_sum, "section", [(s, (s + 1) % sections) for s in range(sections)]
    )
    return (near_sum.astype(F32) + far_sum.astype(F32)).astype(BF16)[None]


def solution(mesh):
    return jax.shard_map(
        shards,
        mesh=mesh,
        in_specs=(
            P("section", "expert", None),
            P("section", None),
            P("section", "expert", None),
            P("section", None),
            P("section", None, None),
            P("section", None),
            P("section", None),
            P("section", None),
            P("section", "expert", None, None),
            P("section", "expert", None, None),
            P("section", "expert", None),
            P("section", "expert", None),
            P("section", None),
        ),
        out_specs=P("section", "expert", None),
        check_vma=False,
    )
```
